32 devices in a mesh: groups: 2 (over y), seq: 4 (over z), tile: 4 (over x, core).
Axes of the slice: x: 2, y: 2, z: 4, core: 2. Of those that a mesh axis runs over, the one named last changes fastest.
Arguments:
- queries: bfloat16 [2048, 8192], P(('groups', 'tile', 'seq')), parts along dimension 0, may hold values from -5 to 5
- keys: bfloat16 [2048, 1024], P(('groups', 'tile', 'seq')), parts along dimension 0, may hold values from -5 to 5
- values: bfloat16 [2048, 1024], P(('groups', 'tile', 'seq')), parts along dimension 0, may hold values from -5 to 5
- block_lists: int32 [128, 8, 16], P(('groups', 'seq'), 'tile'), parts along dimension 0, may hold values from 0 to 7, as said below
- block_counts: int32 [128, 8], P(('groups', 'seq'), 'tile'), parts along dimension 0, may hold values from 1 to 8, as said below
Outputs:
- attended: bfloat16 [2048, 8192], P(('groups', 'tile', 'seq')), parts along dimension 0
The draws below stay inside these ranges and needn't reach their ends.
There are 2 independent parts, one for each index of `groups`. The reference program is written for one: setup_inputs(seed, part) draws one part's arguments, and reference() takes and returns one part's arrays. A program takes and returns all parts, laid end to end along the dimension named above; each array names one. Nothing has to cross between parts.
Inputs may be any that keep to these rules, and one draw needn't show every extreme that they name: `block_lists`: slot 0 of tile q's list is q; slots 1 to block_counts - 1 hold distinct blocks below q; the later slots hold q and are unused. block_counts[h, q] is at most q + 1; some head reads every block in its last tile.
All inputs are finite; a program needn't handle non-finite values.
Results may differ from the reference program's by a relative error of at most 0.0038.
Values may be sent and summed in bfloat16 or wider, within the bound.
No kernel may reach another device: no remote copies, remote signals or barrier semaphores. Data moves between devices by JAX's collectives and lax.ppermute only.
A program may use at most 128 MiB of HBM per device.

```python
import jax
import jax.numpy as jnp
from jax import lax

HQ = 64
KEY_VALUE_HEADS = 8
HEAD_DIMENSION = 128
TILE_ROWS = 128
TOPB = 16
PROMPT_TOKENS = 1024
TILE_TOTAL = 8
GROUP = 8


def selection(key):
    key_caps, key_heavy, key_picks, key_order = jax.random.split(key, 4)
    head_ids = jnp.arange(HQ)
    tiles = jnp.arange(TILE_TOTAL)
    caps = jax.random.randint(key_caps, (HQ,), max(1, TOPB // 4), TOPB + 1)
    heavy = jax.random.randint(key_heavy, (), 0, HQ)
    caps = jnp.where(head_ids == heavy, TOPB, caps)
    lowest = jnp.maximum(caps // 2, 1)
    raw = jax.random.randint(key_picks, (HQ, TILE_TOTAL), 0, 1 << 20)
    picks = lowest[:, None] + raw % (caps - lowest + 1)[:, None]
    counts = jnp.minimum(picks, tiles[None, :] + 1)
    counts = counts.at[:, TILE_TOTAL - 1].set(jnp.minimum(caps, TILE_TOTAL))
    ranks = jax.random.randint(key_order, (HQ, TILE_TOTAL, TILE_TOTAL), 0, 1 << 20) * TILE_TOTAL + tiles[None, None, :]
    below = tiles[None, None, :] < tiles[None, :, None]
    ranks = jnp.where(below, ranks, -1 - tiles[None, None, :])
    taken = min(TOPB - 1, TILE_TOTAL)
    chosen = lax.top_k(ranks, taken)[1].astype(jnp.int32)
    own_tile = jnp.broadcast_to(tiles[None, :, None], (HQ, TILE_TOTAL, 1)).astype(jnp.int32)
    filler = jnp.broadcast_to(tiles[None, :, None], (HQ, TILE_TOTAL, TOPB - 1 - taken)).astype(jnp.int32)
    full_lists = jnp.concatenate([own_tile, chosen, filler], axis=2)
    slot_ids = jnp.arange(TOPB)
    lists = jnp.where(slot_ids[None, None, :] < counts[:, :, None], full_lists, tiles[None, :, None])
    return (lists.astype(jnp.int32), counts.astype(jnp.int32))


def draw_queries(key, part):
    key = jax.random.fold_in(key, 1)
    drawn_result = jnp.clip(jax.random.normal(key, (PROMPT_TOKENS, HQ * HEAD_DIMENSION), jnp.float32), -5.0, 5.0)
    return drawn_result.astype(jnp.bfloat16)


def draw_keys(key, part):
    key = jax.random.fold_in(key, 2)
    drawn_result = jnp.clip(jax.random.normal(key, (PROMPT_TOKENS, KEY_VALUE_HEADS * HEAD_DIMENSION), jnp.float32), -5.0, 5.0)
    return drawn_result.astype(jnp.bfloat16)


def draw_block_lists(key, part):
    lists, counts = selection(key)
    return lists


def draw_block_counts(key, part):
    lists, counts = selection(key)
    return counts


def levels(stream_key, shape, shards, least, top_value):
    factor_of = 1.0
    for position, shards_of in shards:
        heights = jax.random.uniform(jax.random.fold_in(jax.random.fold_in(stream_key, 6), position), (shards_of,), jnp.float32, least / len(shards), top_value / len(shards))
        factor_of = factor_of * jnp.repeat(jnp.exp(heights), shape[position] // shards_of).reshape((-1,) + (1,) * (len(shape) - 1 - position))
    return factor_of


def bell_draw(key, dims, width, most, pieces=(), kind=jnp.bfloat16):
    drawn = width * jax.random.normal(key, dims, jnp.float32)
    if pieces:
        drawn = drawn * levels(key, dims, pieces, -0.22, 0.18)
    return jnp.clip(drawn, -most, most).astype(kind)


def setup_inputs(seed: int = 0, part: int = 0) -> dict:
    key_of = jax.random.split(jax.random.key(seed), 6)
    part_splits = jax.random.split(jax.random.fold_in(key_of[5], part), 6)
    return {
        "queries": draw_queries(jax.random.fold_in(jax.random.fold_in(key_of[5], part), 71), part),
        "keys": draw_keys(jax.random.fold_in(jax.random.fold_in(key_of[5], part), 71), part),
        "values": bell_draw(part_splits[2], (PROMPT_TOKENS, KEY_VALUE_HEADS * HEAD_DIMENSION), 1.0, 5.0, ((0, 16),)),
        "block_lists": draw_block_lists(jax.random.fold_in(jax.random.fold_in(key_of[5], part), 71), part),
        "block_counts": draw_block_counts(jax.random.fold_in(jax.random.fold_in(key_of[5], part), 71), part),
    }


def reference(queries, keys, values, block_lists, block_counts):
    score_scale = HEAD_DIMENSION ** -0.5
    q_tiles = queries.reshape(TILE_TOTAL, TILE_ROWS, HQ, HEAD_DIMENSION)
    key_value_blocks = jnp.stack([keys.reshape(TILE_TOTAL, TILE_ROWS, KEY_VALUE_HEADS, HEAD_DIMENSION), values.reshape(TILE_TOTAL, TILE_ROWS, KEY_VALUE_HEADS, HEAD_DIMENSION)], axis=3)
    kv_heads = (jnp.arange(HQ) // GROUP).astype(jnp.int32)
    slot_ids = jnp.arange(TOPB)
    key_pos = jnp.arange(TILE_ROWS)

    def one_tile(tile_id):
        picked = block_lists[:, tile_id, :]
        used = block_counts[:, tile_id]
        sel_blocks = key_value_blocks[picked, :, kv_heads[:, None]]
        q_block = q_tiles[tile_id].astype(jnp.float32)
        scores = jnp.einsum("qhd,hjkd->hqjk", q_block, sel_blocks[..., 0, :].astype(jnp.float32)) * score_scale
        slot_ok = (slot_ids[None, :] < used[:, None])[:, None, :, None]
        causal = (picked != tile_id)[:, None, :, None] | (key_pos[None, None, None, :] <= key_pos[None, :, None, None])
        kept_mask = slot_ok & causal
        scores = jnp.where(kept_mask, scores, -1e30)
        row_max = jnp.max(scores, axis=(2, 3), keepdims=True)
        probs = jnp.where(kept_mask, jnp.exp(scores - row_max), 0.0)
        totals = jnp.sum(probs, axis=(2, 3))
        probs_low = lax.optimization_barrier(probs.astype(jnp.bfloat16)).astype(jnp.float32)
        mixed = jnp.einsum("hqjk,hjkd->qhd", probs_low, sel_blocks[..., 1, :].astype(jnp.float32))
        mixed = mixed / jnp.transpose(totals)[:, :, None]
        return mixed.astype(jnp.bfloat16)

    attended = lax.map(one_tile, jnp.arange(TILE_TOTAL, dtype=jnp.int32))
    return attended.reshape(PROMPT_TOKENS, HQ * HEAD_DIMENSION)
```

```python
import functools

import jax
import jax.numpy as jnp
from jax import lax
from jax.experimental import pallas as pl
from jax.experimental.pallas import tpu as pltpu
from jax.sharding import Mesh, PartitionSpec as P

HEAD_DIMENSION = 128
TILE_ROWS = 128
GROUP = 8


def attend(q_rows, block_table, block_total, sel_lists_all, sel_counts_all, tile_anchor):
    own_rows, heads_here, head_size = q_rows.shape
    tile_count = sel_lists_all.shape[1]
    slot_total = sel_lists_all.shape[2]
    score_scale = head_size ** (-0.5)
    group_size = 1
    while group_size * TILE_ROWS * heads_here < 512 and tile_count % (2 * group_size) == 0:
        group_size = group_size * 2
    heads_local = jnp.arange(heads_here) // GROUP
    slot_ids = jnp.arange(slot_total)
    key_pos = jnp.arange(TILE_ROWS)

    def one_group(group_id):
        tile_start = group_id * group_size
        q_block = lax.dynamic_slice_in_dim(
            q_rows, tile_start * TILE_ROWS, group_size * TILE_ROWS, 0
        )
        q_block = q_block.reshape(group_size, TILE_ROWS, heads_here, head_size)
        sel_lists = lax.dynamic_slice_in_dim(sel_lists_all, tile_start, group_size, 1)
        sel_counts = lax.dynamic_slice_in_dim(sel_counts_all, tile_start, group_size, 1)
        flat_ids = (heads_local[:, None, None] * block_total + sel_lists).reshape(-1)
        sel_blocks = jnp.take(block_table, flat_ids, axis=0)
        sel_blocks = sel_blocks.reshape(heads_here, group_size, slot_total, TILE_ROWS, 2, head_size)
        scores = (
            jnp.einsum(
                "gqhd,hgjkd->hgqjk",
                q_block,
                sel_blocks[..., 0, :],
                preferred_element_type=jnp.float32,
            )
            * score_scale
        )
        tile_ids = tile_anchor + tile_start + jnp.arange(group_size)
        slot_ok = (slot_ids[None, None, :] < sel_counts[:, :, None])[:, :, None, :, None]
        causal = (sel_lists != tile_ids[None, :, None])[:, :, None, :, None] | (
            key_pos[None, None, None, None, :] <= key_pos[None, None, :, None, None]
        )
        kept_mask = slot_ok & causal
        scores = jnp.where(kept_mask, scores, -1e30)
        row_max = jnp.max(scores, axis=(3, 4), keepdims=True)
        probs = jnp.where(kept_mask, jnp.exp(scores - row_max), 0.0)
        totals = jnp.sum(probs, axis=(3, 4))
        probs_low = probs.astype(jnp.bfloat16)
        mixed = jnp.einsum(
            "hgqjk,hgjkd->gqhd",
            probs_low,
            sel_blocks[..., 1, :],
            preferred_element_type=jnp.float32,
        )
        mixed = mixed / jnp.transpose(totals, (1, 2, 0))[..., None]
        return mixed.astype(jnp.bfloat16)

    attended = lax.map(one_group, jnp.arange(tile_count // group_size, dtype=jnp.int32))
    return attended.reshape(own_rows, heads_here * head_size)


def owner_copies(kv_pairs, owners, heads_here, kv_dev):
    tok_rows, kv_heads_all, pair_width = kv_pairs.shape
    if heads_here >= GROUP:
        return kv_pairs.reshape(tok_rows, owners, kv_dev * pair_width)
    repeats = GROUP // heads_here
    spread = jnp.broadcast_to(
        kv_pairs[:, :, None, :], (tok_rows, kv_heads_all, repeats, pair_width)
    )
    return spread.reshape(tok_rows, owners, kv_dev * pair_width)


def per_device(queries, keys, values, block_lists, block_counts):
    tok_rows = queries.shape[0]
    owners = lax.axis_size("seq")
    heads_here = block_lists.shape[0]
    kv_heads_all = keys.shape[1] // HEAD_DIMENSION
    kv_dev = max(1, heads_here // GROUP)
    q_send = queries.reshape(tok_rows, owners, heads_here * HEAD_DIMENSION)
    kv_pairs = jnp.concatenate(
        [
            keys.reshape(tok_rows, kv_heads_all, HEAD_DIMENSION),
            values.reshape(tok_rows, kv_heads_all, HEAD_DIMENSION),
        ],
        axis=2,
    )
    kv_send = owner_copies(kv_pairs, owners, heads_here, kv_dev)
    q_owned, kv_owned = (
        lax.all_to_all(q_send, "seq", split_axis=1, concat_axis=0, tiled=True),
        lax.all_to_all(kv_send, "seq", split_axis=1, concat_axis=0, tiled=True),
    )
    kv_whole = lax.all_gather(kv_owned, "tile", axis=0, tiled=True)
    key_value_blocks = kv_whole.reshape(-1, TILE_ROWS, kv_dev, 2 * HEAD_DIMENSION)
    block_total = key_value_blocks.shape[0]
    block_table = jnp.transpose(key_value_blocks, (2, 0, 1, 3)).reshape(
        kv_dev * block_total, TILE_ROWS * 2 * HEAD_DIMENSION
    )
    own_rows = q_owned.shape[0]
    q_rows = q_owned.reshape(own_rows, heads_here, HEAD_DIMENSION)
    tile_anchor = lax.axis_index("tile") * block_lists.shape[1]
    attended = attend(q_rows, block_table, block_total, block_lists, block_counts, tile_anchor)
    returned = lax.all_to_all(
        attended.reshape(own_rows, 1, heads_here * HEAD_DIMENSION),
        "seq",
        split_axis=0,
        concat_axis=1,
        tiled=True,
    )
    return returned.reshape(tok_rows, owners * heads_here * HEAD_DIMENSION)


DROP = -1e30
LOG2E = 1.4426950408889634


def ring_steps(z_size):
    chips = 2 * z_size
    places = [(0, p) if p < z_size else (1, chips - 1 - p) for p in range(chips)]

    def device(place, core):
        x, z = places[place % chips]
        return (z * 2 + x) * 2 + core

    ahead = [(device(p, 0), device(p + 1, 0)) for p in range(chips)]
    ahead += [(device(p, 1), device(p - 1, 1)) for p in range(chips)]
    back = [(device(p, 0), device(p - 1, 0)) for p in range(chips)]
    back += [(device(p, 1), device(p + 1, 1)) for p in range(chips)]
    return ahead, back


def ring_kernel(z_size, heads, *refs):
    chips = 2 * z_size
    reach = z_size - 1
    units = refs[2 : 3 + 2 * reach]
    q_own, q_other = refs[0], refs[1]
    k_far, v_far, out_own, out_other, k_aug, v_aug, q_aug, picks = refs[3 + 2 * reach :]
    rows = q_own.shape[0]
    kv_heads = heads // GROUP
    width = HEAD_DIMENSION
    unit_rows = 2 * rows
    x, z, core = lax.axis_index("x"), lax.axis_index("seq"), lax.axis_index("core")
    place = jnp.where(x == 0, z, chips - 1 - z)
    turn = 1 - 2 * core

    def chunk_of(place_from, core_from):
        place_from = lax.rem(place_from + 2 * chips, chips)
        x_from = jnp.where(place_from < z_size, 0, 1)
        z_from = jnp.where(place_from < z_size, place_from, chips - 1 - place_from)
        return (2 * x_from + core_from) * z_size + z_from

    sources = [place]
    sources += [place - step * turn for step in range(1, reach + 1)]
    sources += [place + step * turn for step in range(1, reach + 1)]
    sources += [place + z_size]
    lane = lax.broadcasted_iota(jnp.int32, (rows, width), 1)
    for slot in range(chips):
        for half in range(2):
            mark = jnp.where(lane == chunk_of(sources[slot], jnp.where(half == 0, core, 1 - core)), 1.0, 0.0)
            mark = mark.astype(jnp.bfloat16)
            at = slot * unit_rows + half * rows
            for head in range(kv_heads):
                k_aug[head, at : at + rows, width:] = mark
    ones = jnp.ones((chips * unit_rows, width), jnp.bfloat16)
    for head in range(kv_heads):
        v_aug[head, :, width:] = ones
        columns = slice(head * width, (head + 1) * width)
        for slot in range(chips):
            at = slice(slot * unit_rows, (slot + 1) * unit_rows)
            if slot < chips - 1:
                k_aug[head, at, :width] = units[slot][:unit_rows, columns]
                v_aug[head, at, :width] = units[slot][unit_rows : 2 * unit_rows, columns]
            else:
                k_aug[head, at, :width] = k_far[:, columns]
                v_aug[head, at, :width] = v_far[:, columns]
    for slot in range(chips - 1):
        picks[slot * 16 : slot * 16 + 16, :] = units[slot][2 * unit_rows :, :]

    def slot_of(z_from):
        place_from = jnp.where(x == 0, z_from, chips - 1 - z_from)
        away = lax.rem((place - place_from) * turn + 2 * chips, chips)
        return jnp.where(away < z_size, away, reach + chips - away)

    key_at = lax.broadcasted_iota(jnp.int32, (rows, unit_rows), 1)
    row_at = lax.broadcasted_iota(jnp.int32, (rows, unit_rows), 0)
    lane_row = lax.broadcasted_iota(jnp.int32, (1, width), 1)
    lists_from = heads // 16
    factor = jnp.float32(width**-0.5 * LOG2E)
    for side in (1, 0):
        here = jnp.where(side == 0, core, 1 - core)
        causal = jnp.where(lane_row > chunk_of(place, here), DROP, 0.0)
        key_off = key_at - side * rows
        corner = jnp.where((key_off >= 0) & (key_off < rows) & (key_off > row_at), DROP, 0.0)
        corner = jnp.concatenate([corner] * GROUP, axis=0)
        out = out_own if side == 0 else out_other
        column = pl.multiple_of((side * 2 + z // 2) * width, width)
        for head in range(kv_heads):
            for member in range(GROUP):
                local = head * GROUP + member
                slot = slot_of(core * lists_from + local // 16)
                tile = picks[pl.ds(pl.multiple_of(slot * 16, 16), 16), pl.ds(column, width)]
                bias = tile.astype(jnp.float32)[local % 16 : local % 16 + 1, :] + causal
                at = slice(member * rows, (member + 1) * rows)
                if side == 0:
                    q_from = pl.multiple_of((core * heads + local) * width, width)
                    q_aug[at, :width] = q_own[:, pl.ds(q_from, width)]
                else:
                    q_aug[at, :width] = q_other[:, local * width : (local + 1) * width]
                q_aug[at, width:] = jnp.broadcast_to(bias, (rows, width)).astype(jnp.bfloat16)
            scores = lax.dot_general(
                q_aug[...], k_aug[head], (((1,), (1,)), ((), ())), preferred_element_type=jnp.float32
            )
            scores = jnp.concatenate([scores[:, :unit_rows] + corner, scores[:, unit_rows:]], axis=1)
            row_max = jnp.max(scores, axis=1, keepdims=True)
            probs = jnp.exp2((scores - row_max) * factor).astype(jnp.bfloat16)
            mixed = jnp.dot(probs, v_aug[head], preferred_element_type=jnp.float32)
            result = (mixed[:, :width] / mixed[:, width:]).astype(jnp.bfloat16)
            for member in range(GROUP):
                local = head * GROUP + member
                out[:, local * width : (local + 1) * width] = result[member * rows : (member + 1) * rows]


def per_device_ring(z_size, queries, keys, values, block_lists, block_counts):
    rows = queries.shape[0]
    core = lax.axis_index("core")
    half = keys.shape[1] // 2
    heads = queries.shape[1] // HEAD_DIMENSION // 2
    swap = [(0, 1), (1, 0)]
    ahead, back = ring_steps(z_size)
    axes = ("seq", "x", "core")

    own = core * half
    other = half - own
    lane = jnp.arange(HEAD_DIMENSION) // 2
    slots = jnp.arange(block_lists.shape[2])
    used = (block_lists[..., None] == lane) & (slots < block_counts[..., None])[..., None]
    picks = jnp.where(jnp.any(used, axis=2), 0.0, DROP).astype(jnp.bfloat16)
    picks = picks.reshape(picks.shape[0], 2 * HEAD_DIMENSION)
    sent = jnp.concatenate(
        [
            lax.dynamic_slice_in_dim(keys, other, half, 1),
            lax.dynamic_slice_in_dim(values, other, half, 1),
            jnp.concatenate([picks, picks], axis=1),
        ],
        axis=0,
    )
    got = lax.ppermute(sent, "core", swap)
    unit = jnp.concatenate(
        [
            lax.dynamic_slice_in_dim(keys, own, half, 1),
            got[:rows],
            lax.dynamic_slice_in_dim(values, own, half, 1),
            got[rows : 2 * rows],
            jnp.concatenate([picks, got[2 * rows :, : 2 * HEAD_DIMENSION]], axis=1),
        ],
        axis=0,
    )
    q_width = heads * HEAD_DIMENSION
    q_other = lax.ppermute(
        lax.dynamic_slice_in_dim(queries, q_width - core * q_width, q_width, 1), "core", swap
    )
    one, two, first, second = unit, unit, [], []
    for _ in range(z_size - 1):
        one = lax.ppermute(one, axes, ahead)
        two = lax.ppermute(two, axes, back)
        first.append(one)
        second.append(two)
    unit_rows = 2 * rows
    k_far = lax.ppermute(one[:unit_rows], axes, ahead)
    v_far = lax.ppermute(two[unit_rows : 2 * unit_rows], axes, back)
    chips = 2 * z_size
    kv_heads = heads // GROUP
    out_shape = jax.ShapeDtypeStruct((rows, q_width), jnp.bfloat16)
    kept, away = pl.pallas_call(
        functools.partial(ring_kernel, z_size, heads),
        out_shape=(out_shape, out_shape),
        scratch_shapes=[
            pltpu.VMEM((kv_heads, chips * unit_rows, 2 * HEAD_DIMENSION), jnp.bfloat16),
            pltpu.VMEM((kv_heads, chips * unit_rows, 2 * HEAD_DIMENSION), jnp.bfloat16),
            pltpu.VMEM((GROUP * rows, 2 * HEAD_DIMENSION), jnp.bfloat16),
            pltpu.VMEM((chips * 16, half), jnp.bfloat16),
        ],
        compiler_params=pltpu.CompilerParams(vmem_limit_bytes=40 * 2**20),
        name="attend",
    )(queries, q_other, unit, *first, *second, k_far, v_far)
    back_home = lax.ppermute(away, "core", swap)
    return jnp.where(
        core == 0,
        jnp.concatenate([kept, back_home], axis=1),
        jnp.concatenate([back_home, kept], axis=1),
    )


def solution(mesh):
    groups, z_size, tiles = (mesh.shape[a] for a in ("groups", "seq", "tile"))
    if tiles == 4 and z_size == 4:
        fine = Mesh(mesh.devices.reshape(groups, z_size, 2, 2), ("groups", "seq", "x", "core"))
        step, tile, on = functools.partial(per_device_ring, z_size), ("x", "core"), fine
    else:
        step, tile, on = per_device, ("tile",), mesh
    rows = P(("groups",) + tile + ("seq",), None)
    in_specs = (
        rows,
        rows,
        rows,
        P(("groups", "seq"), tile, None),
        P(("groups", "seq"), tile),
    )
    return jax.shard_map(step, mesh=on, in_specs=in_specs, out_specs=rows, check_vma=False)
```

```python
import functools

import jax
import jax.numpy as jnp
from jax import lax
from jax.experimental import pallas as pl
from jax.experimental.pallas import tpu as pltpu
from jax.sharding import Mesh, PartitionSpec as P

HEAD_DIMENSION = 128
TILE_ROWS = 128
GROUP = 8


def attend(q_rows, block_table, block_total, sel_lists_all, sel_counts_all, tile_anchor):
    own_rows, heads_here, head_size = q_rows.shape
    tile_count = sel_lists_all.shape[1]
    slot_total = sel_lists_all.shape[2]
    score_scale = head_size ** (-0.5)
    group_size = 1
    while group_size * TILE_ROWS * heads_here < 512 and tile_count % (2 * group_size) == 0:
        group_size = group_size * 2
    heads_local = jnp.arange(heads_here) // GROUP
    slot_ids = jnp.arange(slot_total)
    key_pos = jnp.arange(TILE_ROWS)

    def one_group(group_id):
        tile_start = group_id * group_size
        q_block = lax.dynamic_slice_in_dim(
            q_rows, tile_start * TILE_ROWS, group_size * TILE_ROWS, 0
        )
        q_block = q_block.reshape(group_size, TILE_ROWS, heads_here, head_size)
        sel_lists = lax.dynamic_slice_in_dim(sel_lists_all, tile_start, group_size, 1)
        sel_counts = lax.dynamic_slice_in_dim(sel_counts_all, tile_start, group_size, 1)
        flat_ids = (heads_local[:, None, None] * block_total + sel_lists).reshape(-1)
        sel_blocks = jnp.take(block_table, flat_ids, axis=0)
        sel_blocks = sel_blocks.reshape(heads_here, group_size, slot_total, TILE_ROWS, 2, head_size)
        scores = (
            jnp.einsum(
                "gqhd,hgjkd->hgqjk",
                q_block,
                sel_blocks[..., 0, :],
                preferred_element_type=jnp.float32,
            )
            * score_scale
        )
        tile_ids = tile_anchor + tile_start + jnp.arange(group_size)
        slot_ok = (slot_ids[None, None, :] < sel_counts[:, :, None])[:, :, None, :, None]
        causal = (sel_lists != tile_ids[None, :, None])[:, :, None, :, None] | (
            key_pos[None, None, None, None, :] <= key_pos[None, None, :, None, None]
        )
        kept_mask = slot_ok & causal
        scores = jnp.where(kept_mask, scores, -1e30)
        row_max = jnp.max(scores, axis=(3, 4), keepdims=True)
        probs = jnp.where(kept_mask, jnp.exp(scores - row_max), 0.0)
        totals = jnp.sum(probs, axis=(3, 4))
        probs_low = probs.astype(jnp.bfloat16)
        mixed = jnp.einsum(
            "hgqjk,hgjkd->gqhd",
            probs_low,
            sel_blocks[..., 1, :],
            preferred_element_type=jnp.float32,
        )
        mixed = mixed / jnp.transpose(totals, (1, 2, 0))[..., None]
        return mixed.astype(jnp.bfloat16)

    attended = lax.map(one_group, jnp.arange(tile_count // group_size, dtype=jnp.int32))
    return attended.reshape(own_rows, heads_here * head_size)


def owner_copies(kv_pairs, owners, heads_here, kv_dev):
    tok_rows, kv_heads_all, pair_width = kv_pairs.shape
    if heads_here >= GROUP:
        return kv_pairs.reshape(tok_rows, owners, kv_dev * pair_width)
    repeats = GROUP // heads_here
    spread = jnp.broadcast_to(
        kv_pairs[:, :, None, :], (tok_rows, kv_heads_all, repeats, pair_width)
    )
    return spread.reshape(tok_rows, owners, kv_dev * pair_width)


def per_device(queries, keys, values, block_lists, block_counts):
    tok_rows = queries.shape[0]
    owners = lax.axis_size("seq")
    heads_here = block_lists.shape[0]
    kv_heads_all = keys.shape[1] // HEAD_DIMENSION
    kv_dev = max(1, heads_here // GROUP)
    q_send = queries.reshape(tok_rows, owners, heads_here * HEAD_DIMENSION)
    kv_pairs = jnp.concatenate(
        [
            keys.reshape(tok_rows, kv_heads_all, HEAD_DIMENSION),
            values.reshape(tok_rows, kv_heads_all, HEAD_DIMENSION),
        ],
        axis=2,
    )
    kv_send = owner_copies(kv_pairs, owners, heads_here, kv_dev)
    q_owned, kv_owned = (
        lax.all_to_all(q_send, "seq", split_axis=1, concat_axis=0, tiled=True),
        lax.all_to_all(kv_send, "seq", split_axis=1, concat_axis=0, tiled=True),
    )
    kv_whole = lax.all_gather(kv_owned, "tile", axis=0, tiled=True)
    key_value_blocks = kv_whole.reshape(-1, TILE_ROWS, kv_dev, 2 * HEAD_DIMENSION)
    block_total = key_value_blocks.shape[0]
    block_table = jnp.transpose(key_value_blocks, (2, 0, 1, 3)).reshape(
        kv_dev * block_total, TILE_ROWS * 2 * HEAD_DIMENSION
    )
    own_rows = q_owned.shape[0]
    q_rows = q_owned.reshape(own_rows, heads_here, HEAD_DIMENSION)
    tile_anchor = lax.axis_index("tile") * block_lists.shape[1]
    attended = attend(q_rows, block_table, block_total, block_lists, block_counts, tile_anchor)
    returned = lax.all_to_all(
        attended.reshape(own_rows, 1, heads_here * HEAD_DIMENSION),
        "seq",
        split_axis=0,
        concat_axis=1,
        tiled=True,
    )
    return returned.reshape(tok_rows, owners * heads_here * HEAD_DIMENSION)


DROP = -1e30
LOG2E = 1.4426950408889634


def ring_steps(z_size):
    chips = 2 * z_size
    places = [(0, p) if p < z_size else (1, chips - 1 - p) for p in range(chips)]

    def device(place, core):
        x, z = places[place % chips]
        return (z * 2 + x) * 2 + core

    ahead = [(device(p, 0), device(p + 1, 0)) for p in range(chips)]
    ahead += [(device(p, 1), device(p - 1, 1)) for p in range(chips)]
    back = [(device(p, 0), device(p - 1, 0)) for p in range(chips)]
    back += [(device(p, 1), device(p + 1, 1)) for p in range(chips)]
    return ahead, back


def chip_place(z_size):
    x, z = lax.axis_index("x"), lax.axis_index("seq")
    return jnp.where(x == 0, z, 2 * z_size - 1 - z)


def chunk_of(z_size, place, core):
    chips = 2 * z_size
    place = lax.rem(place + 2 * chips, chips)
    x = jnp.where(place < z_size, 0, 1)
    z = jnp.where(place < z_size, place, chips - 1 - place)
    return (2 * x + core) * z_size + z


def fill_keys(z_size, rows, k_aug, v_aug, at, place, keys, values):
    width = HEAD_DIMENSION
    core = lax.axis_index("core")
    lane = lax.broadcasted_iota(jnp.int32, (rows, width), 1)
    for half in range(2):
        chunk = chunk_of(z_size, place, core if half == 0 else 1 - core)
        mark = jnp.where(lane == chunk, 1.0, 0.0).astype(jnp.bfloat16)
        for head in range(k_aug.shape[0]):
            k_aug[head, at + half * rows : at + (half + 1) * rows, width:] = mark
    ones = jnp.ones((2 * rows, width), jnp.bfloat16)
    for head in range(k_aug.shape[0]):
        columns = slice(head * width, (head + 1) * width)
        k_aug[head, at : at + 2 * rows, :width] = keys[:, columns]
        v_aug[head, at : at + 2 * rows, :width] = values[:, columns]
        v_aug[head, at : at + 2 * rows, width:] = ones


def factor():
    return jnp.float32(HEAD_DIMENSION**-0.5 * LOG2E)


def near_kernel(z_size, heads, *refs):
    chips = 2 * z_size
    reach = z_size - 1
    q_own, q_other = refs[:2]
    units = refs[2 : 3 + 2 * reach]
    q_aug, total, top, k_aug, v_aug, lists = refs[3 + 2 * reach :]
    rows = q_own.shape[0]
    width = HEAD_DIMENSION
    unit_rows = 2 * rows
    list_rows = units[0].shape[0] - 2 * unit_rows
    slot_total = 16
    x, z, core = lax.axis_index("x"), lax.axis_index("seq"), lax.axis_index("core")
    place = chip_place(z_size)
    turn = 1 - 2 * core

    sources = [place]
    sources += [place - step * turn for step in range(1, reach + 1)]
    sources += [place + step * turn for step in range(1, reach + 1)]
    for slot, unit in enumerate(units):
        keys, values = unit[:unit_rows, :], unit[unit_rows : 2 * unit_rows, :]
        fill_keys(z_size, rows, k_aug, v_aug, slot * unit_rows, sources[slot], keys, values)
        at = slice(slot * list_rows, (slot + 1) * list_rows)
        lists[at, :] = unit[2 * unit_rows :, :width].astype(jnp.float32)

    def slot_of(z_from):
        place_from = jnp.where(x == 0, z_from, chips - 1 - z_from)
        away = lax.rem((place - place_from) * turn + 2 * chips, chips)
        return jnp.where(away < z_size, away, reach + chips - away)

    key_at = lax.broadcasted_iota(jnp.int32, (rows, unit_rows), 1)
    row_at = lax.broadcasted_iota(jnp.int32, (rows, unit_rows), 0)
    lane = lax.broadcasted_iota(jnp.int32, (list_rows, width), 1)
    block = (lane // 2).astype(jnp.float32)
    spans = heads // list_rows
    for side in (1, 0):
        here = core if side == 0 else 1 - core
        causal = jnp.where(lane > chunk_of(z_size, place, here), DROP, 0.0)
        biases = []
        for span in range(spans):
            slot = slot_of(core * spans + span)
            tile = lists[pl.ds(pl.multiple_of(slot * list_rows, list_rows), list_rows), :]
            hit = jnp.zeros((list_rows, width), jnp.float32)
            for entry in range(slot_total):
                base = side * 2 * slot_total + entry
                picked = jnp.where(
                    z < z_size // 2,
                    tile[:, base : base + 1],
                    tile[:, base + slot_total : base + slot_total + 1],
                )
                hit = jnp.maximum(hit, jnp.where(picked == block, 1.0, 0.0))
            biases.append(jnp.where(hit > 0.0, 0.0, DROP) + causal)
        key_off = key_at - side * rows
        corner = jnp.where((key_off >= 0) & (key_off < rows) & (key_off > row_at), DROP, 0.0)
        corner = jnp.concatenate([corner] * GROUP, axis=0)
        for head in range(heads // GROUP):
            for member in range(GROUP):
                local = head * GROUP + member
                line = local % list_rows
                bias = biases[local // list_rows][line : line + 1, :]
                at = slice(member * rows, (member + 1) * rows)
                if side == 0:
                    q_from = pl.multiple_of((core * heads + local) * width, width)
                    q_aug[side, head, at, :width] = q_own[:, pl.ds(q_from, width)]
                else:
                    q_aug[side, head, at, :width] = q_other[:, local * width : (local + 1) * width]
                q_aug[side, head, at, width:] = jnp.broadcast_to(bias, (rows, width)).astype(jnp.bfloat16)
            scores = lax.dot_general(
                q_aug[side, head], k_aug[head], (((1,), (1,)), ((), ())), preferred_element_type=jnp.float32
            )
            scores = jnp.concatenate([scores[:, :unit_rows] + corner, scores[:, unit_rows:]], axis=1)
            row_max = jnp.max(scores, axis=1, keepdims=True)
            probs = jnp.exp2((scores - row_max) * factor()).astype(jnp.bfloat16)
            total[side, head] = jnp.dot(probs, v_aug[head], preferred_element_type=jnp.float32)
            top[side, head] = jnp.broadcast_to(row_max, (GROUP * rows, width))


def far_kernel(z_size, side, whole, q_aug, total, top, k_far, v_far, out, k_aug, v_aug):
    width = HEAD_DIMENSION
    rows = out.shape[0]
    kv_heads = k_aug.shape[0]
    place = chip_place(z_size) + z_size
    fill_keys(z_size, rows, k_aug, v_aug, 0, place, k_far[...], v_far[...])
    start = lax.axis_index("core") * kv_heads * GROUP * width if whole else 0
    for head in range(kv_heads):
        scores = lax.dot_general(
            q_aug[side, head], k_aug[head], (((1,), (1,)), ((), ())), preferred_element_type=jnp.float32
        )
        near_max = top[side, head]
        row_max = jnp.maximum(near_max, jnp.max(scores, axis=1, keepdims=True))
        shrink = jnp.exp2((near_max - row_max) * factor())
        probs = jnp.exp2((scores - row_max) * factor()).astype(jnp.bfloat16)
        added = jnp.dot(probs, v_aug[head], preferred_element_type=jnp.float32)
        mixed = total[side, head, :, :width] * shrink + added[:, :width]
        sums = total[side, head, :, width:] * shrink + added[:, width:]
        result = (mixed / sums).astype(jnp.bfloat16)
        for member in range(GROUP):
            column = start + (head * GROUP + member) * width
            if whole:
                column = pl.multiple_of(column, width)
            out[:, pl.ds(column, width)] = result[member * rows : (member + 1) * rows]


def per_device_ring(z_size, queries, keys, values, block_lists, block_counts):
    del block_counts
    rows = queries.shape[0]
    core = lax.axis_index("core")
    half = keys.shape[1] // 2
    heads = queries.shape[1] // HEAD_DIMENSION // 2
    swap = [(0, 1), (1, 0)]
    ahead, back = ring_steps(z_size)
    axes = ("seq", "x", "core")

    own = core * half
    k_got = lax.ppermute(keys, "core", swap)
    v_got = lax.ppermute(values, "core", swap)
    l_got = lax.ppermute(block_lists, "core", swap)
    lists = jnp.concatenate([block_lists, l_got], axis=1).astype(jnp.bfloat16)
    lists = lists.reshape(lists.shape[0], lists.shape[1] * lists.shape[2])
    lists = jnp.pad(lists, ((0, 0), (0, half - lists.shape[1])))
    unit = jnp.concatenate(
        [lax.dynamic_slice_in_dim(part, own, half, 1) for part in (keys, k_got, values, v_got)] + [lists],
        axis=0,
    )
    q_width = heads * HEAD_DIMENSION
    late = lax.optimization_barrier((queries, unit))[0]
    q_sent = lax.dynamic_slice_in_dim(late, q_width - core * q_width, q_width, 1)
    q_other = lax.ppermute(q_sent, "core", swap)
    one, two, first, second = unit, unit, [], []
    for _ in range(z_size - 1):
        one = lax.ppermute(one, axes, ahead)
        two = lax.ppermute(two, axes, back)
        first.append(one)
        second.append(two)
    unit_rows = 2 * rows
    k_far = lax.ppermute(one[:unit_rows], axes, ahead)
    v_far = lax.ppermute(two[unit_rows : 2 * unit_rows], axes, back)
    chips = 2 * z_size
    kv_heads = heads // GROUP
    near_rows = (chips - 1) * unit_rows
    group_rows = GROUP * rows
    wide = 2 * HEAD_DIMENSION
    state = pl.pallas_call(
        functools.partial(near_kernel, z_size, heads),
        out_shape=(
            jax.ShapeDtypeStruct((2, kv_heads, group_rows, wide), jnp.bfloat16),
            jax.ShapeDtypeStruct((2, kv_heads, group_rows, wide), jnp.float32),
            jax.ShapeDtypeStruct((2, kv_heads, group_rows, HEAD_DIMENSION), jnp.float32),
        ),
        scratch_shapes=[
            pltpu.VMEM((kv_heads, near_rows, wide), jnp.bfloat16),
            pltpu.VMEM((kv_heads, near_rows, wide), jnp.bfloat16),
            pltpu.VMEM(((chips - 1) * block_lists.shape[0], HEAD_DIMENSION), jnp.float32),
        ],
        compiler_params=pltpu.CompilerParams(vmem_limit_bytes=40 * 2**20),
        cost_estimate=pl.CostEstimate(
            flops=4 * 2 * kv_heads * group_rows * near_rows * wide,
            bytes_accessed=8 * 2**20,
            transcendentals=2 * kv_heads * group_rows * near_rows,
        ),
        name="near",
    )(queries, q_other, unit, *first, *second)

    def finish(side, whole):
        return pl.pallas_call(
            functools.partial(far_kernel, z_size, side, whole),
            out_shape=jax.ShapeDtypeStruct((rows, q_width * (2 if whole else 1)), jnp.bfloat16),
            scratch_shapes=[
                pltpu.VMEM((kv_heads, unit_rows, wide), jnp.bfloat16),
                pltpu.VMEM((kv_heads, unit_rows, wide), jnp.bfloat16),
            ],
            compiler_params=pltpu.CompilerParams(vmem_limit_bytes=40 * 2**20),
            cost_estimate=pl.CostEstimate(
                flops=4 * kv_heads * group_rows * unit_rows * wide,
                bytes_accessed=8 * 2**20,
                transcendentals=2 * kv_heads * group_rows * unit_rows,
            ),
            name="far_own" if whole else "far_other",
        )(*state, k_far, v_far)

    back_home = lax.ppermute(finish(1, False), "core", swap)
    return lax.dynamic_update_slice_in_dim(finish(0, True), back_home, q_width - core * q_width, 1)


def solution(mesh):
    groups, z_size, tiles = (mesh.shape[a] for a in ("groups", "seq", "tile"))
    if tiles == 4 and z_size == 4:
        fine = Mesh(mesh.devices.reshape(groups, z_size, 2, 2), ("groups", "seq", "x", "core"))
        step, tile, on = functools.partial(per_device_ring, z_size), ("x", "core"), fine
    else:
        step, tile, on = per_device, ("tile",), mesh
    rows = P(("groups",) + tile + ("seq",), None)
    in_specs = (
        rows,
        rows,
        rows,
        P(("groups", "seq"), tile, None),
        P(("groups", "seq"), tile),
    )
    return jax.shard_map(step, mesh=on, in_specs=in_specs, out_specs=rows, check_vma=False)
```

```python
import functools

import jax
import jax.numpy as jnp
from jax import lax
from jax.experimental import pallas as pl
from jax.experimental.pallas import tpu as pltpu
from jax.sharding import Mesh, PartitionSpec as P

HEAD_DIMENSION = 128
TILE_ROWS = 128
GROUP = 8


def attend(q_rows, block_table, block_total, sel_lists_all, sel_counts_all, tile_anchor):
    own_rows, heads_here, head_size = q_rows.shape
    tile_count = sel_lists_all.shape[1]
    slot_total = sel_lists_all.shape[2]
    score_scale = head_size ** (-0.5)
    group_size = 1
    while group_size * TILE_ROWS * heads_here < 512 and tile_count % (2 * group_size) == 0:
        group_size = group_size * 2
    heads_local = jnp.arange(heads_here) // GROUP
    slot_ids = jnp.arange(slot_total)
    key_pos = jnp.arange(TILE_ROWS)

    def one_group(group_id):
        tile_start = group_id * group_size
        q_block = lax.dynamic_slice_in_dim(
            q_rows, tile_start * TILE_ROWS, group_size * TILE_ROWS, 0
        )
        q_block = q_block.reshape(group_size, TILE_ROWS, heads_here, head_size)
        sel_lists = lax.dynamic_slice_in_dim(sel_lists_all, tile_start, group_size, 1)
        sel_counts = lax.dynamic_slice_in_dim(sel_counts_all, tile_start, group_size, 1)
        flat_ids = (heads_local[:, None, None] * block_total + sel_lists).reshape(-1)
        sel_blocks = jnp.take(block_table, flat_ids, axis=0)
        sel_blocks = sel_blocks.reshape(heads_here, group_size, slot_total, TILE_ROWS, 2, head_size)
        scores = (
            jnp.einsum(
                "gqhd,hgjkd->hgqjk",
                q_block,
                sel_blocks[..., 0, :],
                preferred_element_type=jnp.float32,
            )
            * score_scale
        )
        tile_ids = tile_anchor + tile_start + jnp.arange(group_size)
        slot_ok = (slot_ids[None, None, :] < sel_counts[:, :, None])[:, :, None, :, None]
        causal = (sel_lists != tile_ids[None, :, None])[:, :, None, :, None] | (
            key_pos[None, None, None, None, :] <= key_pos[None, None, :, None, None]
        )
        kept_mask = slot_ok & causal
        scores = jnp.where(kept_mask, scores, -1e30)
        row_max = jnp.max(scores, axis=(3, 4), keepdims=True)
        probs = jnp.where(kept_mask, jnp.exp(scores - row_max), 0.0)
        totals = jnp.sum(probs, axis=(3, 4))
        probs_low = probs.astype(jnp.bfloat16)
        mixed = jnp.einsum(
            "hgqjk,hgjkd->gqhd",
            probs_low,
            sel_blocks[..., 1, :],
            preferred_element_type=jnp.float32,
        )
        mixed = mixed / jnp.transpose(totals, (1, 2, 0))[..., None]
        return mixed.astype(jnp.bfloat16)

    attended = lax.map(one_group, jnp.arange(tile_count // group_size, dtype=jnp.int32))
    return attended.reshape(own_rows, heads_here * head_size)


def owner_copies(kv_pairs, owners, heads_here, kv_dev):
    tok_rows, kv_heads_all, pair_width = kv_pairs.shape
    if heads_here >= GROUP:
        return kv_pairs.reshape(tok_rows, owners, kv_dev * pair_width)
    repeats = GROUP // heads_here
    spread = jnp.broadcast_to(
        kv_pairs[:, :, None, :], (tok_rows, kv_heads_all, repeats, pair_width)
    )
    return spread.reshape(tok_rows, owners, kv_dev * pair_width)


def per_device(queries, keys, values, block_lists, block_counts):
    tok_rows = queries.shape[0]
    owners = lax.axis_size("seq")
    heads_here = block_lists.shape[0]
    kv_heads_all = keys.shape[1] // HEAD_DIMENSION
    kv_dev = max(1, heads_here // GROUP)
    q_send = queries.reshape(tok_rows, owners, heads_here * HEAD_DIMENSION)
    kv_pairs = jnp.concatenate(
        [
            keys.reshape(tok_rows, kv_heads_all, HEAD_DIMENSION),
            values.reshape(tok_rows, kv_heads_all, HEAD_DIMENSION),
        ],
        axis=2,
    )
    kv_send = owner_copies(kv_pairs, owners, heads_here, kv_dev)
    q_owned, kv_owned = (
        lax.all_to_all(q_send, "seq", split_axis=1, concat_axis=0, tiled=True),
        lax.all_to_all(kv_send, "seq", split_axis=1, concat_axis=0, tiled=True),
    )
    kv_whole = lax.all_gather(kv_owned, "tile", axis=0, tiled=True)
    key_value_blocks = kv_whole.reshape(-1, TILE_ROWS, kv_dev, 2 * HEAD_DIMENSION)
    block_total = key_value_blocks.shape[0]
    block_table = jnp.transpose(key_value_blocks, (2, 0, 1, 3)).reshape(
        kv_dev * block_total, TILE_ROWS * 2 * HEAD_DIMENSION
    )
    own_rows = q_owned.shape[0]
    q_rows = q_owned.reshape(own_rows, heads_here, HEAD_DIMENSION)
    tile_anchor = lax.axis_index("tile") * block_lists.shape[1]
    attended = attend(q_rows, block_table, block_total, block_lists, block_counts, tile_anchor)
    returned = lax.all_to_all(
        attended.reshape(own_rows, 1, heads_here * HEAD_DIMENSION),
        "seq",
        split_axis=0,
        concat_axis=1,
        tiled=True,
    )
    return returned.reshape(tok_rows, owners * heads_here * HEAD_DIMENSION)


DROP = -1e30
LOG2E = 1.4426950408889634


def ring_steps(z_size):
    chips = 2 * z_size
    places = [(0, p) if p < z_size else (1, chips - 1 - p) for p in range(chips)]

    def device(place, core):
        x, z = places[place % chips]
        return (z * 2 + x) * 2 + core

    pairs = [(p, core) for p in range(chips) for core in range(2)]
    ahead = [(device(p, core), device(p + 1, core)) for p, core in pairs]
    back = [(device(p, core), device(p - 1, core)) for p, core in pairs]
    return ahead, back


def chip_place(z_size):
    x, z = lax.axis_index("x"), lax.axis_index("seq")
    return jnp.where(x == 0, z, 2 * z_size - 1 - z)


def chunk_of(z_size, place, core):
    chips = 2 * z_size
    place = lax.rem(place + 2 * chips, chips)
    x = jnp.where(place < z_size, 0, 1)
    z = jnp.where(place < z_size, place, chips - 1 - place)
    return (2 * x + core) * z_size + z


def fill_keys(z_size, rows, k_aug, v_aug, at, place, keys, values):
    width = HEAD_DIMENSION
    core = lax.axis_index("core")
    lane = lax.broadcasted_iota(jnp.int32, (rows, width), 1)
    for half in range(2):
        chunk = chunk_of(z_size, place, core if half == 0 else 1 - core)
        mark = jnp.where(lane == chunk, 1.0, 0.0).astype(jnp.bfloat16)
        for head in range(k_aug.shape[0]):
            k_aug[head, at + half * rows : at + (half + 1) * rows, width:] = mark
    ones = jnp.ones((2 * rows, width), jnp.bfloat16)
    for head in range(k_aug.shape[0]):
        columns = slice(head * width, (head + 1) * width)
        k_aug[head, at : at + 2 * rows, :width] = keys[:, columns]
        v_aug[head, at : at + 2 * rows, :width] = values[:, columns]
        v_aug[head, at : at + 2 * rows, width:] = ones


def factor():
    return jnp.float32(HEAD_DIMENSION**-0.5 * LOG2E)


def near_kernel(z_size, heads, *refs):
    chips = 2 * z_size
    reach = z_size - 1
    near = 1 + 2 * reach
    q_own, q_other = refs[:2]
    k_units, v_units = refs[2 : 2 + near], refs[2 + near : 2 + 2 * near]
    q_aug, total, top, k_aug, v_aug, lists = refs[2 + 2 * near :]
    rows = q_own.shape[0]
    width = HEAD_DIMENSION
    unit_rows = 2 * rows
    list_rows = v_units[0].shape[0] - unit_rows
    slot_total = 16
    x, z, core = lax.axis_index("x"), lax.axis_index("seq"), lax.axis_index("core")
    place = chip_place(z_size)

    sources = [place]
    sources += [place - step for step in range(1, reach + 1)]
    sources += [place + step for step in range(1, reach + 1)]
    for slot in range(near):
        keys, values = k_units[slot][...], v_units[slot][:unit_rows, :]
        fill_keys(z_size, rows, k_aug, v_aug, slot * unit_rows, sources[slot], keys, values)
        at = slice(slot * list_rows, (slot + 1) * list_rows)
        lists[at, :] = v_units[slot][unit_rows:, :width].astype(jnp.float32)

    def slot_of(z_from):
        place_from = jnp.where(x == 0, z_from, chips - 1 - z_from)
        away = lax.rem(place - place_from + chips, chips)
        return jnp.where(away < z_size, away, reach + chips - away)

    key_at = lax.broadcasted_iota(jnp.int32, (rows, unit_rows), 1)
    row_at = lax.broadcasted_iota(jnp.int32, (rows, unit_rows), 0)
    lane = lax.broadcasted_iota(jnp.int32, (list_rows, width), 1)
    block = (lane // 2).astype(jnp.float32)
    spans = heads // list_rows
    for side in (1, 0):
        here = core if side == 0 else 1 - core
        causal = jnp.where(lane > chunk_of(z_size, place, here), DROP, 0.0)
        biases = []
        for span in range(spans):
            slot = slot_of(core * spans + span)
            tile = lists[pl.ds(pl.multiple_of(slot * list_rows, list_rows), list_rows), :]
            hit = jnp.zeros((list_rows, width), jnp.float32)
            for entry in range(slot_total):
                base = side * 2 * slot_total + entry
                picked = jnp.where(
                    z < z_size // 2,
                    tile[:, base : base + 1],
                    tile[:, base + slot_total : base + slot_total + 1],
                )
                hit = jnp.maximum(hit, jnp.where(picked == block, 1.0, 0.0))
            biases.append(jnp.where(hit > 0.0, 0.0, DROP) + causal)
        key_off = key_at - side * rows
        corner = jnp.where((key_off >= 0) & (key_off < rows) & (key_off > row_at), DROP, 0.0)
        corner = jnp.concatenate([corner] * GROUP, axis=0)
        for head in range(heads // GROUP):
            for member in range(GROUP):
                local = head * GROUP + member
                line = local % list_rows
                bias = biases[local // list_rows][line : line + 1, :]
                at = slice(member * rows, (member + 1) * rows)
                if side == 0:
                    q_from = pl.multiple_of((core * heads + local) * width, width)
                    q_aug[side, head, at, :width] = q_own[:, pl.ds(q_from, width)]
                else:
                    q_aug[side, head, at, :width] = q_other[:, local * width : (local + 1) * width]
                q_aug[side, head, at, width:] = jnp.broadcast_to(bias, (rows, width)).astype(jnp.bfloat16)
            scores = lax.dot_general(
                q_aug[side, head], k_aug[head], (((1,), (1,)), ((), ())), preferred_element_type=jnp.float32
            )
            scores = jnp.concatenate([scores[:, :unit_rows] + corner, scores[:, unit_rows:]], axis=1)
            row_max = jnp.max(scores, axis=1, keepdims=True)
            probs = jnp.exp2((scores - row_max) * factor()).astype(jnp.bfloat16)
            total[side, head] = jnp.dot(probs, v_aug[head], preferred_element_type=jnp.float32)
            top[side, head] = jnp.broadcast_to(row_max, (GROUP * rows, width))


def far_kernel(z_size, side, whole, q_aug, total, top, k_far, v_far, out, k_aug, v_aug):
    width = HEAD_DIMENSION
    rows = out.shape[0]
    kv_heads = k_aug.shape[0]
    place = chip_place(z_size) + z_size
    fill_keys(z_size, rows, k_aug, v_aug, 0, place, k_far[...], v_far[...])
    start = lax.axis_index("core") * kv_heads * GROUP * width if whole else 0
    for head in range(kv_heads):
        scores = lax.dot_general(
            q_aug[side, head], k_aug[head], (((1,), (1,)), ((), ())), preferred_element_type=jnp.float32
        )
        near_max = top[side, head]
        row_max = jnp.maximum(near_max, jnp.max(scores, axis=1, keepdims=True))
        shrink = jnp.exp2((near_max - row_max) * factor())
        probs = jnp.exp2((scores - row_max) * factor()).astype(jnp.bfloat16)
        added = jnp.dot(probs, v_aug[head], preferred_element_type=jnp.float32)
        mixed = total[side, head, :, :width] * shrink + added[:, :width]
        sums = total[side, head, :, width:] * shrink + added[:, width:]
        result = (mixed / sums).astype(jnp.bfloat16)
        for member in range(GROUP):
            column = start + (head * GROUP + member) * width
            if whole:
                column = pl.multiple_of(column, width)
            out[:, pl.ds(column, width)] = result[member * rows : (member + 1) * rows]


def per_device_ring(z_size, queries, keys, values, block_lists, block_counts):
    del block_counts
    rows = queries.shape[0]
    core = lax.axis_index("core")
    half = keys.shape[1] // 2
    heads = queries.shape[1] // HEAD_DIMENSION // 2
    swap = [(0, 1), (1, 0)]
    ahead, back = ring_steps(z_size)
    axes = ("seq", "x", "core")

    own = core * half
    k_got = lax.ppermute(keys, "core", swap)
    v_got = lax.ppermute(values, "core", swap)
    l_got = lax.ppermute(block_lists, "core", swap)
    lists = jnp.concatenate([block_lists, l_got], axis=1).astype(jnp.bfloat16)
    lists = lists.reshape(lists.shape[0], lists.shape[1] * lists.shape[2])
    lists = jnp.pad(lists, ((0, 0), (0, half - lists.shape[1])))
    def halves(part, got):
        return [lax.dynamic_slice_in_dim(part, own, half, 1), lax.dynamic_slice_in_dim(got, own, half, 1)]

    k_unit = jnp.concatenate(halves(keys, k_got), axis=0)
    v_unit = jnp.concatenate(halves(values, v_got) + [lists], axis=0)
    q_width = heads * HEAD_DIMENSION
    q_sent = lax.dynamic_slice_in_dim(queries, q_width - core * q_width, q_width, 1)
    q_other = lax.ppermute(q_sent, "core", swap)
    k_unit, q_other = lax.optimization_barrier((k_unit, q_other))
    k_ahead, k_back, v_ahead, v_back = [k_unit], [k_unit], [v_unit], [v_unit]
    for _ in range(z_size - 1):
        k_ahead.append(lax.ppermute(k_ahead[-1], axes, ahead))
        k_back.append(lax.ppermute(k_back[-1], axes, back))
        v_ahead.append(lax.ppermute(v_ahead[-1], axes, ahead))
        v_back.append(lax.ppermute(v_back[-1], axes, back))
    unit_rows = 2 * rows
    k_far = lax.ppermute(k_ahead[-1], axes, ahead)
    v_far = lax.ppermute(v_back[-1][:unit_rows], axes, back)
    chips = 2 * z_size
    kv_heads = heads // GROUP
    near_rows = (chips - 1) * unit_rows
    group_rows = GROUP * rows
    wide = 2 * HEAD_DIMENSION
    state = pl.pallas_call(
        functools.partial(near_kernel, z_size, heads),
        out_shape=(
            jax.ShapeDtypeStruct((2, kv_heads, group_rows, wide), jnp.bfloat16),
            jax.ShapeDtypeStruct((2, kv_heads, group_rows, wide), jnp.float32),
            jax.ShapeDtypeStruct((2, kv_heads, group_rows, HEAD_DIMENSION), jnp.float32),
        ),
        scratch_shapes=[
            pltpu.VMEM((kv_heads, near_rows, wide), jnp.bfloat16),
            pltpu.VMEM((kv_heads, near_rows, wide), jnp.bfloat16),
            pltpu.VMEM(((chips - 1) * block_lists.shape[0], HEAD_DIMENSION), jnp.float32),
        ],
        compiler_params=pltpu.CompilerParams(vmem_limit_bytes=40 * 2**20),
        cost_estimate=pl.CostEstimate(
            flops=4 * 2 * kv_heads * group_rows * near_rows * wide,
            bytes_accessed=8 * 2**20,
            transcendentals=2 * kv_heads * group_rows * near_rows,
        ),
        name="near",
    )(queries, q_other, *k_ahead, *k_back[1:], *v_ahead, *v_back[1:])

    def finish(side, whole):
        return pl.pallas_call(
            functools.partial(far_kernel, z_size, side, whole),
            out_shape=jax.ShapeDtypeStruct((rows, q_width * (2 if whole else 1)), jnp.bfloat16),
            scratch_shapes=[
                pltpu.VMEM((kv_heads, unit_rows, wide), jnp.bfloat16),
                pltpu.VMEM((kv_heads, unit_rows, wide), jnp.bfloat16),
            ],
            compiler_params=pltpu.CompilerParams(vmem_limit_bytes=40 * 2**20),
            cost_estimate=pl.CostEstimate(
                flops=4 * kv_heads * group_rows * unit_rows * wide,
                bytes_accessed=8 * 2**20,
                transcendentals=2 * kv_heads * group_rows * unit_rows,
            ),
            name="far_own" if whole else "far_other",
        )(*state, k_far, v_far)

    back_home = lax.ppermute(finish(1, False), "core", swap)
    return lax.dynamic_update_slice_in_dim(finish(0, True), back_home, q_width - core * q_width, 1)


def solution(mesh):
    groups, z_size, tiles = (mesh.shape[a] for a in ("groups", "seq", "tile"))
    if tiles == 4 and z_size == 4:
        fine = Mesh(mesh.devices.reshape(groups, z_size, 2, 2), ("groups", "seq", "x", "core"))
        step, tile, on = functools.partial(per_device_ring, z_size), ("x", "core"), fine
    else:
        step, tile, on = per_device, ("tile",), mesh
    rows = P(("groups",) + tile + ("seq",), None)
    in_specs = (
        rows,
        rows,
        rows,
        P(("groups", "seq"), tile, None),
        P(("groups", "seq"), tile),
    )
    return jax.shard_map(step, mesh=on, in_specs=in_specs, out_specs=rows, check_vma=False)
```

```python
import functools

import jax
import jax.numpy as jnp
from jax import lax
from jax.experimental import pallas as pl
from jax.experimental.pallas import tpu as pltpu
from jax.sharding import Mesh, PartitionSpec as P

HEAD_DIMENSION = 128
TILE_ROWS = 128
GROUP = 8


def attend(q_rows, block_table, block_total, sel_lists_all, sel_counts_all, tile_anchor):
    own_rows, heads_here, head_size = q_rows.shape
    tile_count = sel_lists_all.shape[1]
    slot_total = sel_lists_all.shape[2]
    score_scale = head_size ** (-0.5)
    group_size = 1
    while group_size * TILE_ROWS * heads_here < 512 and tile_count % (2 * group_size) == 0:
        group_size = group_size * 2
    heads_local = jnp.arange(heads_here) // GROUP
    slot_ids = jnp.arange(slot_total)
    key_pos = jnp.arange(TILE_ROWS)

    def one_group(group_id):
        tile_start = group_id * group_size
        q_block = lax.dynamic_slice_in_dim(
            q_rows, tile_start * TILE_ROWS, group_size * TILE_ROWS, 0
        )
        q_block = q_block.reshape(group_size, TILE_ROWS, heads_here, head_size)
        sel_lists = lax.dynamic_slice_in_dim(sel_lists_all, tile_start, group_size, 1)
        sel_counts = lax.dynamic_slice_in_dim(sel_counts_all, tile_start, group_size, 1)
        flat_ids = (heads_local[:, None, None] * block_total + sel_lists).reshape(-1)
        sel_blocks = jnp.take(block_table, flat_ids, axis=0)
        sel_blocks = sel_blocks.reshape(heads_here, group_size, slot_total, TILE_ROWS, 2, head_size)
        scores = (
            jnp.einsum(
                "gqhd,hgjkd->hgqjk",
                q_block,
                sel_blocks[..., 0, :],
                preferred_element_type=jnp.float32,
            )
            * score_scale
        )
        tile_ids = tile_anchor + tile_start + jnp.arange(group_size)
        slot_ok = (slot_ids[None, None, :] < sel_counts[:, :, None])[:, :, None, :, None]
        causal = (sel_lists != tile_ids[None, :, None])[:, :, None, :, None] | (
            key_pos[None, None, None, None, :] <= key_pos[None, None, :, None, None]
        )
        kept_mask = slot_ok & causal
        scores = jnp.where(kept_mask, scores, -1e30)
        row_max = jnp.max(scores, axis=(3, 4), keepdims=True)
        probs = jnp.where(kept_mask, jnp.exp(scores - row_max), 0.0)
        totals = jnp.sum(probs, axis=(3, 4))
        probs_low = probs.astype(jnp.bfloat16)
        mixed = jnp.einsum(
            "hgqjk,hgjkd->gqhd",
            probs_low,
            sel_blocks[..., 1, :],
            preferred_element_type=jnp.float32,
        )
        mixed = mixed / jnp.transpose(totals, (1, 2, 0))[..., None]
        return mixed.astype(jnp.bfloat16)

    attended = lax.map(one_group, jnp.arange(tile_count // group_size, dtype=jnp.int32))
    return attended.reshape(own_rows, heads_here * head_size)


def owner_copies(kv_pairs, owners, heads_here, kv_dev):
    tok_rows, kv_heads_all, pair_width = kv_pairs.shape
    if heads_here >= GROUP:
        return kv_pairs.reshape(tok_rows, owners, kv_dev * pair_width)
    repeats = GROUP // heads_here
    spread = jnp.broadcast_to(
        kv_pairs[:, :, None, :], (tok_rows, kv_heads_all, repeats, pair_width)
    )
    return spread.reshape(tok_rows, owners, kv_dev * pair_width)


def per_device(queries, keys, values, block_lists, block_counts):
    tok_rows = queries.shape[0]
    owners = lax.axis_size("seq")
    heads_here = block_lists.shape[0]
    kv_heads_all = keys.shape[1] // HEAD_DIMENSION
    kv_dev = max(1, heads_here // GROUP)
    q_send = queries.reshape(tok_rows, owners, heads_here * HEAD_DIMENSION)
    kv_pairs = jnp.concatenate(
        [
            keys.reshape(tok_rows, kv_heads_all, HEAD_DIMENSION),
            values.reshape(tok_rows, kv_heads_all, HEAD_DIMENSION),
        ],
        axis=2,
    )
    kv_send = owner_copies(kv_pairs, owners, heads_here, kv_dev)
    q_owned, kv_owned = (
        lax.all_to_all(q_send, "seq", split_axis=1, concat_axis=0, tiled=True),
        lax.all_to_all(kv_send, "seq", split_axis=1, concat_axis=0, tiled=True),
    )
    kv_whole = lax.all_gather(kv_owned, "tile", axis=0, tiled=True)
    key_value_blocks = kv_whole.reshape(-1, TILE_ROWS, kv_dev, 2 * HEAD_DIMENSION)
    block_total = key_value_blocks.shape[0]
    block_table = jnp.transpose(key_value_blocks, (2, 0, 1, 3)).reshape(
        kv_dev * block_total, TILE_ROWS * 2 * HEAD_DIMENSION
    )
    own_rows = q_owned.shape[0]
    q_rows = q_owned.reshape(own_rows, heads_here, HEAD_DIMENSION)
    tile_anchor = lax.axis_index("tile") * block_lists.shape[1]
    attended = attend(q_rows, block_table, block_total, block_lists, block_counts, tile_anchor)
    returned = lax.all_to_all(
        attended.reshape(own_rows, 1, heads_here * HEAD_DIMENSION),
        "seq",
        split_axis=0,
        concat_axis=1,
        tiled=True,
    )
    return returned.reshape(tok_rows, owners * heads_here * HEAD_DIMENSION)


DROP = -1e30
LOG2E = 1.4426950408889634


def ring_steps(z_size):
    chips = 2 * z_size
    places = [(0, p) if p < z_size else (1, chips - 1 - p) for p in range(chips)]

    def device(place, core):
        x, z = places[place % chips]
        return (z * 2 + x) * 2 + core

    pairs = [(p, core) for p in range(chips) for core in range(2)]
    ahead = [(device(p, core), device(p + 1, core)) for p, core in pairs]
    back = [(device(p, core), device(p - 1, core)) for p, core in pairs]
    return ahead, back


def chip_place(z_size):
    x, z = lax.axis_index("x"), lax.axis_index("seq")
    return jnp.where(x == 0, z, 2 * z_size - 1 - z)


def chunk_of(z_size, place, core):
    chips = 2 * z_size
    place = lax.rem(place + 2 * chips, chips)
    x = jnp.where(place < z_size, 0, 1)
    z = jnp.where(place < z_size, place, chips - 1 - place)
    return (2 * x + core) * z_size + z


def fill_keys(z_size, rows, k_aug, v_aug, at, place, keys, values):
    width = HEAD_DIMENSION
    core = lax.axis_index("core")
    lane = lax.broadcasted_iota(jnp.int32, (rows, width), 1)
    for half in range(2):
        chunk = chunk_of(z_size, place, core if half == 0 else 1 - core)
        mark = jnp.where(lane == chunk, 1.0, 0.0).astype(jnp.bfloat16)
        for head in range(k_aug.shape[0]):
            k_aug[head, at + half * rows : at + (half + 1) * rows, width:] = mark
    ones = jnp.ones((2 * rows, width), jnp.bfloat16)
    for head in range(k_aug.shape[0]):
        columns = slice(head * width, (head + 1) * width)
        k_aug[head, at : at + 2 * rows, :width] = keys[:, columns]
        v_aug[head, at : at + 2 * rows, :width] = values[:, columns]
        v_aug[head, at : at + 2 * rows, width:] = ones


def factor():
    return jnp.float32(HEAD_DIMENSION**-0.5 * LOG2E)


def near_kernel(z_size, heads, *refs):
    chips = 2 * z_size
    reach = z_size - 1
    near = 1 + 2 * reach
    q_own, q_other = refs[:2]
    k_units, v_units = refs[2 : 2 + near], refs[2 + near : 2 + 2 * near]
    states = refs[2 + 2 * near : 8 + 2 * near]
    k_aug, v_aug, lists = refs[8 + 2 * near : 11 + 2 * near]
    rows = q_own.shape[0]
    width = HEAD_DIMENSION
    unit_rows = 2 * rows
    list_rows = v_units[0].shape[0] - unit_rows
    slot_total = 16
    x, z, core = lax.axis_index("x"), lax.axis_index("seq"), lax.axis_index("core")
    place = chip_place(z_size)

    sources = [place]
    sources += [place - step for step in range(1, reach + 1)]
    sources += [place + step for step in range(1, reach + 1)]
    for slot in range(near):
        keys, values = k_units[slot][...], v_units[slot][:unit_rows, :]
        fill_keys(z_size, rows, k_aug, v_aug, slot * unit_rows, sources[slot], keys, values)
        at = slice(slot * list_rows, (slot + 1) * list_rows)
        lists[at, :] = v_units[slot][unit_rows:, :width].astype(jnp.float32)

    def slot_of(z_from):
        place_from = jnp.where(x == 0, z_from, chips - 1 - z_from)
        away = lax.rem(place - place_from + chips, chips)
        return jnp.where(away < z_size, away, reach + chips - away)

    key_at = lax.broadcasted_iota(jnp.int32, (rows, unit_rows), 1)
    row_at = lax.broadcasted_iota(jnp.int32, (rows, unit_rows), 0)
    lane = lax.broadcasted_iota(jnp.int32, (list_rows, width), 1)
    block = (lane // 2).astype(jnp.float32)
    spans = heads // list_rows
    def settle(side, head, scores, corner):
        part_rows = GROUP * rows // 2
        for part in range(2):
            at = slice(part * part_rows, (part + 1) * part_rows)
            first = scores[at, :unit_rows] + corner[at]
            row_max = jnp.max(
                jnp.maximum(first, best_of(scores[at, unit_rows:], unit_rows)), axis=1, keepdims=True
            )
            probs = [jnp.exp2((first - row_max) * factor()).astype(jnp.bfloat16)]
            probs.append(jnp.exp2((scores[at, unit_rows:] - row_max) * factor()).astype(jnp.bfloat16))
            probs = jnp.concatenate(probs, axis=1)
            states[3 * side + 1][head, at] = jnp.dot(
                probs, v_aug[head], preferred_element_type=jnp.float32
            )
            states[3 * side + 2][head, at] = jnp.broadcast_to(row_max, (part_rows, width))

    def best_of(block, step):
        best = block[:, :step]
        for start in range(step, block.shape[1], step):
            best = jnp.maximum(best, block[:, start : start + step])
        return best

    waiting = ()
    for side in (1, 0):
        here = core if side == 0 else 1 - core
        q_aug = states[3 * side]
        causal = jnp.where(lane > chunk_of(z_size, place, here), DROP, 0.0)
        biases = []
        for span in range(spans):
            slot = slot_of(core * spans + span)
            tile = lists[pl.ds(pl.multiple_of(slot * list_rows, list_rows), list_rows), :]
            hit = jnp.zeros((list_rows, width), jnp.float32)
            for entry in range(slot_total):
                base = side * 2 * slot_total + entry
                picked = jnp.where(
                    z < z_size // 2,
                    tile[:, base : base + 1],
                    tile[:, base + slot_total : base + slot_total + 1],
                )
                hit = jnp.maximum(hit, jnp.where(picked == block, 1.0, 0.0))
            biases.append(jnp.where(hit > 0.0, 0.0, DROP) + causal)
        key_off = key_at - side * rows
        corner = jnp.where((key_off >= 0) & (key_off < rows) & (key_off > row_at), DROP, 0.0)
        corner = jnp.concatenate([corner] * GROUP, axis=0)
        for head in range(heads // GROUP):
            for member in range(GROUP):
                local = head * GROUP + member
                line = local % list_rows
                bias = biases[local // list_rows][line : line + 1, :]
                at = slice(member * rows, (member + 1) * rows)
                if side == 0:
                    q_from = pl.multiple_of((core * heads + local) * width, width)
                    q_aug[head, at, :width] = q_own[:, pl.ds(q_from, width)]
                else:
                    q_aug[head, at, :width] = q_other[:, local * width : (local + 1) * width]
                q_aug[head, at, width:] = jnp.broadcast_to(bias, (rows, width)).astype(jnp.bfloat16)
            scores = lax.dot_general(
                q_aug[head], k_aug[head], (((1,), (1,)), ((), ())), preferred_element_type=jnp.float32
            )
            if waiting:
                settle(*waiting)
            waiting = (side, head, scores, corner)
    settle(*waiting)


def far_kernel(z_size, whole, q_aug, total, top, k_far, v_far, target, k_aug, v_aug, *spare):
    width = HEAD_DIMENSION
    rows = target.shape[0]
    out = spare[0] if whole else target
    copies = []
    kv_heads = k_aug.shape[0]
    place = chip_place(z_size) + z_size
    fill_keys(z_size, rows, k_aug, v_aug, 0, place, k_far[...], v_far[...])
    for head in range(kv_heads):
        scores = lax.dot_general(
            q_aug[head], k_aug[head], (((1,), (1,)), ((), ())), preferred_element_type=jnp.float32
        )
        near_max = top[head]
        row_max = jnp.maximum(near_max, jnp.max(scores, axis=1, keepdims=True))
        shrink = jnp.exp2((near_max - row_max) * factor())
        probs = jnp.exp2((scores - row_max) * factor()).astype(jnp.bfloat16)
        added = jnp.dot(probs, v_aug[head], preferred_element_type=jnp.float32)
        mixed = total[head, :, :width] * shrink + added[:, :width]
        sums = total[head, :, width:] * shrink + added[:, width:]
        result = (mixed / sums).astype(jnp.bfloat16)
        for member in range(GROUP):
            column = (head * GROUP + member) * width
            out[:, column : column + width] = result[member * rows : (member + 1) * rows]
        if whole:
            span = GROUP * width
            start = pl.multiple_of((lax.axis_index("core") * kv_heads + head) * span, span)
            copy = pltpu.make_async_copy(
                out.at[:, pl.ds(head * span, span)], target.at[:, pl.ds(start, span)], spare[1].at[head]
            )
            copy.start()
            copies.append(copy)
    for copy in copies:
        copy.wait()


def per_device_ring(z_size, queries, keys, values, block_lists, block_counts):
    del block_counts
    rows = queries.shape[0]
    core = lax.axis_index("core")
    half = keys.shape[1] // 2
    heads = queries.shape[1] // HEAD_DIMENSION // 2
    swap = [(0, 1), (1, 0)]
    ahead, back = ring_steps(z_size)
    axes = ("seq", "x", "core")

    own = core * half
    k_got = lax.ppermute(keys, "core", swap)
    v_got = lax.ppermute(values, "core", swap)
    l_got = lax.ppermute(block_lists, "core", swap)
    lines = [part[:, tile] for part in (block_lists, l_got) for tile in range(block_lists.shape[1])]
    lists = jnp.concatenate(lines, axis=1).astype(jnp.bfloat16)
    lists = jnp.pad(lists, ((0, 0), (0, half - lists.shape[1])))
    def halves(part, got):
        return [lax.dynamic_slice_in_dim(part, own, half, 1), lax.dynamic_slice_in_dim(got, own, half, 1)]

    k_unit = jnp.concatenate(halves(keys, k_got), axis=0)
    v_unit = jnp.concatenate(halves(values, v_got) + [lists], axis=0)
    q_width = heads * HEAD_DIMENSION
    q_sent = lax.dynamic_slice_in_dim(queries, q_width - core * q_width, q_width, 1)
    q_other = lax.ppermute(q_sent, "core", swap)
    k_unit, q_other = lax.optimization_barrier((k_unit, q_other))
    k_ahead, k_back, v_ahead, v_back = [k_unit], [k_unit], [v_unit], [v_unit]
    for _ in range(z_size - 1):
        k_ahead.append(lax.ppermute(k_ahead[-1], axes, ahead))
        k_back.append(lax.ppermute(k_back[-1], axes, back))
        v_ahead.append(lax.ppermute(v_ahead[-1], axes, ahead))
        v_back.append(lax.ppermute(v_back[-1], axes, back))
    unit_rows = 2 * rows
    k_far = lax.ppermute(k_ahead[-1], axes, ahead)
    v_far = lax.ppermute(v_back[-1][:unit_rows], axes, back)
    chips = 2 * z_size
    kv_heads = heads // GROUP
    near_rows = (chips - 1) * unit_rows
    group_rows = GROUP * rows
    wide = 2 * HEAD_DIMENSION
    state = pl.pallas_call(
        functools.partial(near_kernel, z_size, heads),
        out_shape=(
            jax.ShapeDtypeStruct((kv_heads, group_rows, wide), jnp.bfloat16),
            jax.ShapeDtypeStruct((kv_heads, group_rows, wide), jnp.float32),
            jax.ShapeDtypeStruct((kv_heads, group_rows, HEAD_DIMENSION), jnp.float32),
        )
        * 2,
        scratch_shapes=[
            pltpu.VMEM((kv_heads, near_rows, wide), jnp.bfloat16),
            pltpu.VMEM((kv_heads, near_rows, wide), jnp.bfloat16),
            pltpu.VMEM(((chips - 1) * block_lists.shape[0], HEAD_DIMENSION), jnp.float32),
        ],
        compiler_params=pltpu.CompilerParams(vmem_limit_bytes=40 * 2**20),
        cost_estimate=pl.CostEstimate(
            flops=4 * 2 * kv_heads * group_rows * near_rows * wide,
            bytes_accessed=8 * 2**20,
            transcendentals=2 * kv_heads * group_rows * near_rows,
        ),
        name="near",
    )(queries, q_other, *k_ahead, *k_back[1:], *v_ahead, *v_back[1:])

    def finish(side, whole):
        return pl.pallas_call(
            functools.partial(far_kernel, z_size, whole),
            out_shape=jax.ShapeDtypeStruct((rows, q_width * (2 if whole else 1)), jnp.bfloat16),
            out_specs=pl.BlockSpec(memory_space=pl.ANY if whole else pltpu.VMEM),
            scratch_shapes=[
                pltpu.VMEM((kv_heads, unit_rows, wide), jnp.bfloat16),
                pltpu.VMEM((kv_heads, unit_rows, wide), jnp.bfloat16),
            ]
            + ([pltpu.VMEM((rows, q_width), jnp.bfloat16), pltpu.SemaphoreType.DMA((kv_heads,))] if whole else []),
            compiler_params=pltpu.CompilerParams(vmem_limit_bytes=40 * 2**20),
            cost_estimate=pl.CostEstimate(
                flops=4 * kv_heads * group_rows * unit_rows * wide,
                bytes_accessed=8 * 2**20,
                transcendentals=2 * kv_heads * group_rows * unit_rows,
            ),
            name="far_own" if whole else "far_other",
        )(*state[3 * side : 3 * side + 3], k_far, v_far)

    back_home = lax.ppermute(finish(1, False), "core", swap)
    return lax.dynamic_update_slice_in_dim(finish(0, True), back_home, q_width - core * q_width, 1)


def solution(mesh):
    groups, z_size, tiles = (mesh.shape[a] for a in ("groups", "seq", "tile"))
    if tiles == 4 and z_size == 4:
        fine = Mesh(mesh.devices.reshape(groups, z_size, 2, 2), ("groups", "seq", "x", "core"))
        step, tile, on = functools.partial(per_device_ring, z_size), ("x", "core"), fine
    else:
        step, tile, on = per_device, ("tile",), mesh
    rows = P(("groups",) + tile + ("seq",), None)
    in_specs = (
        rows,
        rows,
        rows,
        P(("groups", "seq"), tile, None),
        P(("groups", "seq"), tile),
    )
    return jax.shard_map(step, mesh=on, in_specs=in_specs, out_specs=rows, check_vma=False)
```

```python
import functools

import jax
import jax.numpy as jnp
from jax import lax
from jax.experimental import pallas as pl
from jax.experimental.pallas import tpu as pltpu
from jax.sharding import Mesh, PartitionSpec as P

HEAD_DIMENSION = 128
TILE_ROWS = 128
GROUP = 8


def attend(q_rows, block_table, block_total, sel_lists_all, sel_counts_all, tile_anchor):
    own_rows, heads_here, head_size = q_rows.shape
    tile_count = sel_lists_all.shape[1]
    slot_total = sel_lists_all.shape[2]
    score_scale = head_size ** (-0.5)
    group_size = 1
    while group_size * TILE_ROWS * heads_here < 512 and tile_count % (2 * group_size) == 0:
        group_size = group_size * 2
    heads_local = jnp.arange(heads_here) // GROUP
    slot_ids = jnp.arange(slot_total)
    key_pos = jnp.arange(TILE_ROWS)

    def one_group(group_id):
        tile_start = group_id * group_size
        q_block = lax.dynamic_slice_in_dim(
            q_rows, tile_start * TILE_ROWS, group_size * TILE_ROWS, 0
        )
        q_block = q_block.reshape(group_size, TILE_ROWS, heads_here, head_size)
        sel_lists = lax.dynamic_slice_in_dim(sel_lists_all, tile_start, group_size, 1)
        sel_counts = lax.dynamic_slice_in_dim(sel_counts_all, tile_start, group_size, 1)
        flat_ids = (heads_local[:, None, None] * block_total + sel_lists).reshape(-1)
        sel_blocks = jnp.take(block_table, flat_ids, axis=0)
        sel_blocks = sel_blocks.reshape(heads_here, group_size, slot_total, TILE_ROWS, 2, head_size)
        scores = (
            jnp.einsum(
                "gqhd,hgjkd->hgqjk",
                q_block,
                sel_blocks[..., 0, :],
                preferred_element_type=jnp.float32,
            )
            * score_scale
        )
        tile_ids = tile_anchor + tile_start + jnp.arange(group_size)
        slot_ok = (slot_ids[None, None, :] < sel_counts[:, :, None])[:, :, None, :, None]
        causal = (sel_lists != tile_ids[None, :, None])[:, :, None, :, None] | (
            key_pos[None, None, None, None, :] <= key_pos[None, None, :, None, None]
        )
        kept_mask = slot_ok & causal
        scores = jnp.where(kept_mask, scores, -1e30)
        row_max = jnp.max(scores, axis=(3, 4), keepdims=True)
        probs = jnp.where(kept_mask, jnp.exp(scores - row_max), 0.0)
        totals = jnp.sum(probs, axis=(3, 4))
        probs_low = probs.astype(jnp.bfloat16)
        mixed = jnp.einsum(
            "hgqjk,hgjkd->gqhd",
            probs_low,
            sel_blocks[..., 1, :],
            preferred_element_type=jnp.float32,
        )
        mixed = mixed / jnp.transpose(totals, (1, 2, 0))[..., None]
        return mixed.astype(jnp.bfloat16)

    attended = lax.map(one_group, jnp.arange(tile_count // group_size, dtype=jnp.int32))
    return attended.reshape(own_rows, heads_here * head_size)


def owner_copies(kv_pairs, owners, heads_here, kv_dev):
    tok_rows, kv_heads_all, pair_width = kv_pairs.shape
    if heads_here >= GROUP:
        return kv_pairs.reshape(tok_rows, owners, kv_dev * pair_width)
    repeats = GROUP // heads_here
    spread = jnp.broadcast_to(
        kv_pairs[:, :, None, :], (tok_rows, kv_heads_all, repeats, pair_width)
    )
    return spread.reshape(tok_rows, owners, kv_dev * pair_width)


def per_device(queries, keys, values, block_lists, block_counts):
    tok_rows = queries.shape[0]
    owners = lax.axis_size("seq")
    heads_here = block_lists.shape[0]
    kv_heads_all = keys.shape[1] // HEAD_DIMENSION
    kv_dev = max(1, heads_here // GROUP)
    q_send = queries.reshape(tok_rows, owners, heads_here * HEAD_DIMENSION)
    kv_pairs = jnp.concatenate(
        [
            keys.reshape(tok_rows, kv_heads_all, HEAD_DIMENSION),
            values.reshape(tok_rows, kv_heads_all, HEAD_DIMENSION),
        ],
        axis=2,
    )
    kv_send = owner_copies(kv_pairs, owners, heads_here, kv_dev)
    q_owned, kv_owned = (
        lax.all_to_all(q_send, "seq", split_axis=1, concat_axis=0, tiled=True),
        lax.all_to_all(kv_send, "seq", split_axis=1, concat_axis=0, tiled=True),
    )
    kv_whole = lax.all_gather(kv_owned, "tile", axis=0, tiled=True)
    key_value_blocks = kv_whole.reshape(-1, TILE_ROWS, kv_dev, 2 * HEAD_DIMENSION)
    block_total = key_value_blocks.shape[0]
    block_table = jnp.transpose(key_value_blocks, (2, 0, 1, 3)).reshape(
        kv_dev * block_total, TILE_ROWS * 2 * HEAD_DIMENSION
    )
    own_rows = q_owned.shape[0]
    q_rows = q_owned.reshape(own_rows, heads_here, HEAD_DIMENSION)
    tile_anchor = lax.axis_index("tile") * block_lists.shape[1]
    attended = attend(q_rows, block_table, block_total, block_lists, block_counts, tile_anchor)
    returned = lax.all_to_all(
        attended.reshape(own_rows, 1, heads_here * HEAD_DIMENSION),
        "seq",
        split_axis=0,
        concat_axis=1,
        tiled=True,
    )
    return returned.reshape(tok_rows, owners * heads_here * HEAD_DIMENSION)


DROP = -1e30
LOG2E = 1.4426950408889634


def ring_steps(z_size):
    chips = 2 * z_size
    places = [(0, p) if p < z_size else (1, chips - 1 - p) for p in range(chips)]

    def device(place, core):
        x, z = places[place % chips]
        return (z * 2 + x) * 2 + core

    pairs = [(p, core) for p in range(chips) for core in range(2)]
    ahead = [(device(p, core), device(p + 1, core)) for p, core in pairs]
    back = [(device(p, core), device(p - 1, core)) for p, core in pairs]
    return ahead, back


def chip_place(z_size):
    x, z = lax.axis_index("x"), lax.axis_index("seq")
    return jnp.where(x == 0, z, 2 * z_size - 1 - z)


def chunk_of(z_size, place, core):
    chips = 2 * z_size
    place = lax.rem(place + 2 * chips, chips)
    x = jnp.where(place < z_size, 0, 1)
    z = jnp.where(place < z_size, place, chips - 1 - place)
    return (2 * x + core) * z_size + z


def fill_keys(z_size, rows, k_aug, v_aug, at, place, keys, values):
    width = HEAD_DIMENSION
    core = lax.axis_index("core")
    lane = lax.broadcasted_iota(jnp.int32, (rows, width), 1)
    for half in range(2):
        chunk = chunk_of(z_size, place, core if half == 0 else 1 - core)
        mark = jnp.where(lane == chunk, 1.0, 0.0).astype(jnp.bfloat16)
        for head in range(k_aug.shape[0]):
            k_aug[head, at + half * rows : at + (half + 1) * rows, width:] = mark
    ones = jnp.ones((2 * rows, width), jnp.bfloat16)
    for head in range(k_aug.shape[0]):
        columns = slice(head * width, (head + 1) * width)
        k_aug[head, at : at + 2 * rows, :width] = keys[:, columns]
        v_aug[head, at : at + 2 * rows, :width] = values[:, columns]
        v_aug[head, at : at + 2 * rows, width:] = ones


def factor():
    return jnp.float32(HEAD_DIMENSION**-0.5 * LOG2E)


def near_kernel(z_size, heads, *refs):
    chips = 2 * z_size
    reach = z_size - 1
    near = 1 + 2 * reach
    q_own, q_other = refs[:2]
    k_units, v_units = refs[2 : 2 + near], refs[2 + near : 2 + 2 * near]
    states = refs[2 + 2 * near : 8 + 2 * near]
    k_aug, v_aug, lists = refs[8 + 2 * near : 11 + 2 * near]
    rows = q_own.shape[0]
    width = HEAD_DIMENSION
    unit_rows = 2 * rows
    list_rows = v_units[0].shape[0] - unit_rows
    slot_total = 16
    x, z, core = lax.axis_index("x"), lax.axis_index("seq"), lax.axis_index("core")
    place = chip_place(z_size)

    sources = [place]
    sources += [place - step for step in range(1, reach + 1)]
    sources += [place + step for step in range(1, reach + 1)]
    for slot in range(near):
        keys, values = k_units[slot][...], v_units[slot][:unit_rows, :]
        fill_keys(z_size, rows, k_aug, v_aug, slot * unit_rows, sources[slot], keys, values)
        at = slice(slot * list_rows, (slot + 1) * list_rows)
        lists[at, :] = v_units[slot][unit_rows:, :width].astype(jnp.float32)

    def slot_of(z_from):
        place_from = jnp.where(x == 0, z_from, chips - 1 - z_from)
        away = lax.rem(place - place_from + chips, chips)
        return jnp.where(away < z_size, away, reach + chips - away)

    key_at = lax.broadcasted_iota(jnp.int32, (rows, unit_rows), 1)
    row_at = lax.broadcasted_iota(jnp.int32, (rows, unit_rows), 0)
    lane = lax.broadcasted_iota(jnp.int32, (list_rows, width), 1)
    block = (lane // 2).astype(jnp.float32)
    spans = heads // list_rows
    def settle(side, head, scores, corner):
        part_rows = GROUP * rows // 2
        for part in range(2):
            at = slice(part * part_rows, (part + 1) * part_rows)
            first = scores[at, :unit_rows] + corner[at]
            row_max = jnp.max(
                jnp.maximum(first, best_of(scores[at, unit_rows:], unit_rows)), axis=1, keepdims=True
            )
            probs = [jnp.exp2((first - row_max) * factor()).astype(jnp.bfloat16)]
            probs.append(jnp.exp2((scores[at, unit_rows:] - row_max) * factor()).astype(jnp.bfloat16))
            probs = jnp.concatenate(probs, axis=1)
            states[3 * side + 1][head, at] = jnp.dot(
                probs, v_aug[head], preferred_element_type=jnp.float32
            )
            states[3 * side + 2][head, at] = jnp.broadcast_to(row_max, (part_rows, width))

    def best_of(block, step):
        best = block[:, :step]
        for start in range(step, block.shape[1], step):
            best = jnp.maximum(best, block[:, start : start + step])
        return best

    waiting = ()
    for side in (1, 0):
        here = core if side == 0 else 1 - core
        q_aug = states[3 * side]
        causal = jnp.where(lane > chunk_of(z_size, place, here), DROP, 0.0)
        biases = []
        for span in range(spans):
            slot = slot_of(core * spans + span)
            tile = lists[pl.ds(pl.multiple_of(slot * list_rows, list_rows), list_rows), :]
            hit = jnp.zeros((list_rows, width), jnp.float32)
            for entry in range(slot_total):
                base = side * 2 * slot_total + entry
                picked = jnp.where(
                    z < z_size // 2,
                    tile[:, base : base + 1],
                    tile[:, base + slot_total : base + slot_total + 1],
                )
                hit = jnp.maximum(hit, jnp.where(picked == block, 1.0, 0.0))
            biases.append(jnp.where(hit > 0.0, 0.0, DROP) + causal)
        key_off = key_at - side * rows
        corner = jnp.where((key_off >= 0) & (key_off < rows) & (key_off > row_at), DROP, 0.0)
        corner = jnp.concatenate([corner] * GROUP, axis=0)
        for head in range(heads // GROUP):
            for member in range(GROUP):
                local = head * GROUP + member
                line = local % list_rows
                bias = biases[local // list_rows][line : line + 1, :]
                at = slice(member * rows, (member + 1) * rows)
                if side == 0:
                    q_from = pl.multiple_of((core * heads + local) * width, width)
                    q_aug[head, at, :width] = q_own[:, pl.ds(q_from, width)]
                else:
                    q_aug[head, at, :width] = q_other[:, local * width : (local + 1) * width]
                q_aug[head, at, width:] = jnp.broadcast_to(bias, (rows, width)).astype(jnp.bfloat16)
            scores = lax.dot_general(
                q_aug[head], k_aug[head], (((1,), (1,)), ((), ())), preferred_element_type=jnp.float32
            )
            if waiting:
                settle(*waiting)
            waiting = (side, head, scores, corner)
    settle(*waiting)


def far_kernel(z_size, whole, q_aug, total, top, k_far, v_far, target, k_aug, v_aug, *spare):
    width = HEAD_DIMENSION
    rows = target.shape[0]
    out = spare[0] if whole else target
    copies = []
    kv_heads = k_aug.shape[0]
    place = chip_place(z_size) + z_size
    fill_keys(z_size, rows, k_aug, v_aug, 0, place, k_far[...], v_far[...])
    for head in range(kv_heads):
        scores = lax.dot_general(
            q_aug[head], k_aug[head], (((1,), (1,)), ((), ())), preferred_element_type=jnp.float32
        )
        near_max = top[head]
        row_max = jnp.maximum(near_max, jnp.max(scores, axis=1, keepdims=True))
        shrink = jnp.exp2((near_max - row_max) * factor())
        probs = jnp.exp2((scores - row_max) * factor()).astype(jnp.bfloat16)
        added = jnp.dot(probs, v_aug[head], preferred_element_type=jnp.float32)
        mixed = total[head, :, :width] * shrink + added[:, :width]
        sums = total[head, :, width:] * shrink + added[:, width:]
        result = (mixed / sums).astype(jnp.bfloat16)
        for member in range(GROUP):
            column = (head * GROUP + member) * width
            out[:, column : column + width] = result[member * rows : (member + 1) * rows]
        if whole:
            span = GROUP * width
            start = pl.multiple_of((lax.axis_index("core") * kv_heads + head) * span, span)
            copy = pltpu.make_async_copy(
                out.at[:, pl.ds(head * span, span)], target.at[:, pl.ds(start, span)], spare[1].at[head]
            )
            copy.start()
            copies.append(copy)
    for copy in copies:
        copy.wait()


def join_kernel(half_done, got, out, sem):
    del half_done
    span = got.shape[1]
    start = pl.multiple_of((1 - lax.axis_index("core")) * span, span)
    copy = pltpu.make_async_copy(got, out.at[:, pl.ds(start, span)], sem)
    copy.start()
    copy.wait()


def per_device_ring(z_size, queries, keys, values, block_lists, block_counts):
    del block_counts
    rows = queries.shape[0]
    core = lax.axis_index("core")
    half = keys.shape[1] // 2
    heads = queries.shape[1] // HEAD_DIMENSION // 2
    swap = [(0, 1), (1, 0)]
    ahead, back = ring_steps(z_size)
    axes = ("seq", "x", "core")

    own = core * half
    k_got = lax.ppermute(keys, "core", swap)
    v_got = lax.ppermute(values, "core", swap)
    l_got = lax.ppermute(block_lists, "core", swap)
    lines = [part[:, tile] for part in (block_lists, l_got) for tile in range(block_lists.shape[1])]
    lists = jnp.concatenate(lines, axis=1).astype(jnp.bfloat16)
    lists = jnp.pad(lists, ((0, 0), (0, half - lists.shape[1])))
    def halves(part, got):
        return [lax.dynamic_slice_in_dim(part, own, half, 1), lax.dynamic_slice_in_dim(got, own, half, 1)]

    k_unit = jnp.concatenate(halves(keys, k_got), axis=0)
    v_unit = jnp.concatenate(halves(values, v_got) + [lists], axis=0)
    q_width = heads * HEAD_DIMENSION
    q_sent = lax.dynamic_slice_in_dim(queries, q_width - core * q_width, q_width, 1)
    q_other = lax.ppermute(q_sent, "core", swap)
    k_unit, q_other = lax.optimization_barrier((k_unit, q_other))
    k_ahead, k_back, v_ahead, v_back = [k_unit], [k_unit], [v_unit], [v_unit]
    for _ in range(z_size - 1):
        k_ahead.append(lax.ppermute(k_ahead[-1], axes, ahead))
        v_ahead.append(lax.ppermute(v_ahead[-1], axes, ahead))
        k_back.append(lax.ppermute(k_back[-1], axes, back))
        v_back.append(lax.ppermute(v_back[-1], axes, back))
    unit_rows = 2 * rows
    k_far = lax.ppermute(k_ahead[-1], axes, ahead)
    v_far = lax.ppermute(v_back[-1][:unit_rows], axes, back)
    chips = 2 * z_size
    kv_heads = heads // GROUP
    near_rows = (chips - 1) * unit_rows
    group_rows = GROUP * rows
    wide = 2 * HEAD_DIMENSION
    state = pl.pallas_call(
        functools.partial(near_kernel, z_size, heads),
        out_shape=(
            jax.ShapeDtypeStruct((kv_heads, group_rows, wide), jnp.bfloat16),
            jax.ShapeDtypeStruct((kv_heads, group_rows, wide), jnp.float32),
            jax.ShapeDtypeStruct((kv_heads, group_rows, HEAD_DIMENSION), jnp.float32),
        )
        * 2,
        scratch_shapes=[
            pltpu.VMEM((kv_heads, near_rows, wide), jnp.bfloat16),
            pltpu.VMEM((kv_heads, near_rows, wide), jnp.bfloat16),
            pltpu.VMEM(((chips - 1) * block_lists.shape[0], HEAD_DIMENSION), jnp.float32),
        ],
        compiler_params=pltpu.CompilerParams(vmem_limit_bytes=40 * 2**20),
        cost_estimate=pl.CostEstimate(
            flops=4 * 2 * kv_heads * group_rows * near_rows * wide,
            bytes_accessed=8 * 2**20,
            transcendentals=2 * kv_heads * group_rows * near_rows,
        ),
        name="near",
    )(queries, q_other, *k_ahead, *k_back[1:], *v_ahead, *v_back[1:])

    def finish(side, whole):
        return pl.pallas_call(
            functools.partial(far_kernel, z_size, whole),
            out_shape=jax.ShapeDtypeStruct((rows, q_width * (2 if whole else 1)), jnp.bfloat16),
            out_specs=pl.BlockSpec(memory_space=pl.ANY if whole else pltpu.VMEM),
            scratch_shapes=[
                pltpu.VMEM((kv_heads, unit_rows, wide), jnp.bfloat16),
                pltpu.VMEM((kv_heads, unit_rows, wide), jnp.bfloat16),
            ]
            + ([pltpu.VMEM((rows, q_width), jnp.bfloat16), pltpu.SemaphoreType.DMA((kv_heads,))] if whole else []),
            compiler_params=pltpu.CompilerParams(vmem_limit_bytes=30 * 2**20),
            cost_estimate=pl.CostEstimate(
                flops=4 * kv_heads * group_rows * unit_rows * wide,
                bytes_accessed=8 * 2**20,
                transcendentals=2 * kv_heads * group_rows * unit_rows,
            ),
            name="far_own" if whole else "far_other",
        )(*state[3 * side : 3 * side + 3], k_far, v_far)

    back_home = lax.ppermute(finish(1, False), "core", swap)
    return pl.pallas_call(
        join_kernel,
        out_shape=jax.ShapeDtypeStruct((rows, 2 * q_width), jnp.bfloat16),
        in_specs=[pl.BlockSpec(memory_space=pl.ANY)] * 2,
        out_specs=pl.BlockSpec(memory_space=pl.ANY),
        scratch_shapes=[pltpu.SemaphoreType.DMA],
        input_output_aliases={0: 0},
        compiler_params=pltpu.CompilerParams(vmem_limit_bytes=30 * 2**20),
        name="join",
    )(finish(0, True), back_home)


def solution(mesh):
    groups, z_size, tiles = (mesh.shape[a] for a in ("groups", "seq", "tile"))
    if tiles == 4 and z_size == 4:
        fine = Mesh(mesh.devices.reshape(groups, z_size, 2, 2), ("groups", "seq", "x", "core"))
        step, tile, on = functools.partial(per_device_ring, z_size), ("x", "core"), fine
    else:
        step, tile, on = per_device, ("tile",), mesh
    rows = P(("groups",) + tile + ("seq",), None)
    in_specs = (
        rows,
        rows,
        rows,
        P(("groups", "seq"), tile, None),
        P(("groups", "seq"), tile),
    )
    return jax.shard_map(step, mesh=on, in_specs=in_specs, out_specs=rows, check_vma=False)
```

```python
import functools

import jax
import jax.numpy as jnp
from jax import lax
from jax.experimental import pallas as pl
from jax.experimental.pallas import tpu as pltpu
from jax.sharding import Mesh, PartitionSpec as P

HEAD_DIMENSION = 128
TILE_ROWS = 128
GROUP = 8


def attend(q_rows, block_table, block_total, sel_lists_all, sel_counts_all, tile_anchor):
    own_rows, heads_here, head_size = q_rows.shape
    tile_count = sel_lists_all.shape[1]
    slot_total = sel_lists_all.shape[2]
    score_scale = head_size ** (-0.5)
    group_size = 1
    while group_size * TILE_ROWS * heads_here < 512 and tile_count % (2 * group_size) == 0:
        group_size = group_size * 2
    heads_local = jnp.arange(heads_here) // GROUP
    slot_ids = jnp.arange(slot_total)
    key_pos = jnp.arange(TILE_ROWS)

    def one_group(group_id):
        tile_start = group_id * group_size
        q_block = lax.dynamic_slice_in_dim(
            q_rows, tile_start * TILE_ROWS, group_size * TILE_ROWS, 0
        )
        q_block = q_block.reshape(group_size, TILE_ROWS, heads_here, head_size)
        sel_lists = lax.dynamic_slice_in_dim(sel_lists_all, tile_start, group_size, 1)
        sel_counts = lax.dynamic_slice_in_dim(sel_counts_all, tile_start, group_size, 1)
        flat_ids = (heads_local[:, None, None] * block_total + sel_lists).reshape(-1)
        sel_blocks = jnp.take(block_table, flat_ids, axis=0)
        sel_blocks = sel_blocks.reshape(heads_here, group_size, slot_total, TILE_ROWS, 2, head_size)
        scores = (
            jnp.einsum(
                "gqhd,hgjkd->hgqjk",
                q_block,
                sel_blocks[..., 0, :],
                preferred_element_type=jnp.float32,
            )
            * score_scale
        )
        tile_ids = tile_anchor + tile_start + jnp.arange(group_size)
        slot_ok = (slot_ids[None, None, :] < sel_counts[:, :, None])[:, :, None, :, None]
        causal = (sel_lists != tile_ids[None, :, None])[:, :, None, :, None] | (
            key_pos[None, None, None, None, :] <= key_pos[None, None, :, None, None]
        )
        kept_mask = slot_ok & causal
        scores = jnp.where(kept_mask, scores, -1e30)
        row_max = jnp.max(scores, axis=(3, 4), keepdims=True)
        probs = jnp.where(kept_mask, jnp.exp(scores - row_max), 0.0)
        totals = jnp.sum(probs, axis=(3, 4))
        probs_low = probs.astype(jnp.bfloat16)
        mixed = jnp.einsum(
            "hgqjk,hgjkd->gqhd",
            probs_low,
            sel_blocks[..., 1, :],
            preferred_element_type=jnp.float32,
        )
        mixed = mixed / jnp.transpose(totals, (1, 2, 0))[..., None]
        return mixed.astype(jnp.bfloat16)

    attended = lax.map(one_group, jnp.arange(tile_count // group_size, dtype=jnp.int32))
    return attended.reshape(own_rows, heads_here * head_size)


def owner_copies(kv_pairs, owners, heads_here, kv_dev):
    tok_rows, kv_heads_all, pair_width = kv_pairs.shape
    if heads_here >= GROUP:
        return kv_pairs.reshape(tok_rows, owners, kv_dev * pair_width)
    repeats = GROUP // heads_here
    spread = jnp.broadcast_to(
        kv_pairs[:, :, None, :], (tok_rows, kv_heads_all, repeats, pair_width)
    )
    return spread.reshape(tok_rows, owners, kv_dev * pair_width)


def per_device(queries, keys, values, block_lists, block_counts):
    tok_rows = queries.shape[0]
    owners = lax.axis_size("seq")
    heads_here = block_lists.shape[0]
    kv_heads_all = keys.shape[1] // HEAD_DIMENSION
    kv_dev = max(1, heads_here // GROUP)
    q_send = queries.reshape(tok_rows, owners, heads_here * HEAD_DIMENSION)
    kv_pairs = jnp.concatenate(
        [
            keys.reshape(tok_rows, kv_heads_all, HEAD_DIMENSION),
            values.reshape(tok_rows, kv_heads_all, HEAD_DIMENSION),
        ],
        axis=2,
    )
    kv_send = owner_copies(kv_pairs, owners, heads_here, kv_dev)
    q_owned, kv_owned = (
        lax.all_to_all(q_send, "seq", split_axis=1, concat_axis=0, tiled=True),
        lax.all_to_all(kv_send, "seq", split_axis=1, concat_axis=0, tiled=True),
    )
    kv_whole = lax.all_gather(kv_owned, "tile", axis=0, tiled=True)
    key_value_blocks = kv_whole.reshape(-1, TILE_ROWS, kv_dev, 2 * HEAD_DIMENSION)
    block_total = key_value_blocks.shape[0]
    block_table = jnp.transpose(key_value_blocks, (2, 0, 1, 3)).reshape(
        kv_dev * block_total, TILE_ROWS * 2 * HEAD_DIMENSION
    )
    own_rows = q_owned.shape[0]
    q_rows = q_owned.reshape(own_rows, heads_here, HEAD_DIMENSION)
    tile_anchor = lax.axis_index("tile") * block_lists.shape[1]
    attended = attend(q_rows, block_table, block_total, block_lists, block_counts, tile_anchor)
    returned = lax.all_to_all(
        attended.reshape(own_rows, 1, heads_here * HEAD_DIMENSION),
        "seq",
        split_axis=0,
        concat_axis=1,
        tiled=True,
    )
    return returned.reshape(tok_rows, owners * heads_here * HEAD_DIMENSION)


DROP = -1e30
LOG2E = 1.4426950408889634


def ring_steps(z_size):
    chips = 2 * z_size
    places = [(0, p) if p < z_size else (1, chips - 1 - p) for p in range(chips)]

    def device(place, core):
        x, z = places[place % chips]
        return (z * 2 + x) * 2 + core

    pairs = [(p, core) for p in range(chips) for core in range(2)]
    ahead = [(device(p, core), device(p + 1, core)) for p, core in pairs]
    back = [(device(p, core), device(p - 1, core)) for p, core in pairs]
    return ahead, back


def chip_place(z_size):
    x, z = lax.axis_index("x"), lax.axis_index("seq")
    return jnp.where(x == 0, z, 2 * z_size - 1 - z)


def chunk_of(z_size, place, core):
    chips = 2 * z_size
    place = lax.rem(place + 2 * chips, chips)
    x = jnp.where(place < z_size, 0, 1)
    z = jnp.where(place < z_size, place, chips - 1 - place)
    return (2 * x + core) * z_size + z


def fill_keys(z_size, rows, k_aug, v_aug, at, place, keys, values):
    width = HEAD_DIMENSION
    core = lax.axis_index("core")
    lane = lax.broadcasted_iota(jnp.int32, (rows, width), 1)
    for half in range(2):
        chunk = chunk_of(z_size, place, core if half == 0 else 1 - core)
        mark = jnp.where(lane == chunk, 1.0, 0.0).astype(jnp.bfloat16)
        for head in range(k_aug.shape[0]):
            k_aug[head, at + half * rows : at + (half + 1) * rows, width:] = mark
    ones = jnp.ones((2 * rows, width), jnp.bfloat16)
    for head in range(k_aug.shape[0]):
        columns = slice(head * width, (head + 1) * width)
        k_aug[head, at : at + 2 * rows, :width] = keys[:, columns]
        v_aug[head, at : at + 2 * rows, :width] = values[:, columns]
        v_aug[head, at : at + 2 * rows, width:] = ones


def factor():
    return jnp.float32(HEAD_DIMENSION**-0.5 * LOG2E)


def near_kernel(z_size, heads, *refs):
    chips = 2 * z_size
    reach = z_size - 1
    near = 1 + 2 * reach
    q_own, q_other = refs[:2]
    k_units, v_units = refs[2 : 2 + near], refs[2 + near : 2 + 2 * near]
    states = refs[2 + 2 * near : 8 + 2 * near]
    k_aug, v_aug, lists = refs[8 + 2 * near : 11 + 2 * near]
    rows = q_own.shape[0]
    width = HEAD_DIMENSION
    unit_rows = 2 * rows
    list_rows = v_units[0].shape[0] - unit_rows
    slot_total = 16
    x, z, core = lax.axis_index("x"), lax.axis_index("seq"), lax.axis_index("core")
    place = chip_place(z_size)

    sources = [place]
    sources += [place - step for step in range(1, reach + 1)]
    sources += [place + step for step in range(1, reach + 1)]
    for slot in range(near):
        keys, values = k_units[slot][...], v_units[slot][:unit_rows, :]
        fill_keys(z_size, rows, k_aug, v_aug, slot * unit_rows, sources[slot], keys, values)
        at = slice(slot * list_rows, (slot + 1) * list_rows)
        lists[at, :] = v_units[slot][unit_rows:, :width].astype(jnp.float32)

    def slot_of(z_from):
        place_from = jnp.where(x == 0, z_from, chips - 1 - z_from)
        away = lax.rem(place - place_from + chips, chips)
        return jnp.where(away < z_size, away, reach + chips - away)

    key_at = lax.broadcasted_iota(jnp.int32, (rows, unit_rows), 1)
    row_at = lax.broadcasted_iota(jnp.int32, (rows, unit_rows), 0)
    lane = lax.broadcasted_iota(jnp.int32, (list_rows, width), 1)
    block = (lane // 2).astype(jnp.float32)
    spans = heads // list_rows
    def settle(side, head, scores, corner):
        part_rows = GROUP * rows // 2
        for part in range(2):
            at = slice(part * part_rows, (part + 1) * part_rows)
            first = scores[at, :unit_rows] + corner[at]
            row_max = jnp.max(
                jnp.maximum(first, best_of(scores[at, unit_rows:], unit_rows)), axis=1, keepdims=True
            )
            probs = [jnp.exp2((first - row_max) * factor()).astype(jnp.bfloat16)]
            probs.append(jnp.exp2((scores[at, unit_rows:] - row_max) * factor()).astype(jnp.bfloat16))
            probs = jnp.concatenate(probs, axis=1)
            states[3 * side + 1][head, at] = jnp.dot(
                probs, v_aug[head], preferred_element_type=jnp.float32
            )
            states[3 * side + 2][head, at] = jnp.broadcast_to(row_max, (part_rows, width))

    def best_of(block, step):
        best = block[:, :step]
        for start in range(step, block.shape[1], step):
            best = jnp.maximum(best, block[:, start : start + step])
        return best

    waiting = ()
    for side in (1, 0):
        here = core if side == 0 else 1 - core
        q_aug = states[3 * side]
        causal = jnp.where(lane > chunk_of(z_size, place, here), DROP, 0.0)
        biases = []
        for span in range(spans):
            slot = slot_of(core * spans + span)
            tile = lists[pl.ds(pl.multiple_of(slot * list_rows, list_rows), list_rows), :]
            hit = jnp.zeros((list_rows, width), jnp.float32)
            for entry in range(slot_total):
                base = side * 2 * slot_total + entry
                picked = jnp.where(
                    z < z_size // 2,
                    tile[:, base : base + 1],
                    tile[:, base + slot_total : base + slot_total + 1],
                )
                hit = jnp.maximum(hit, jnp.where(picked == block, 1.0, 0.0))
            biases.append(jnp.where(hit > 0.0, 0.0, DROP) + causal)
        key_off = key_at - side * rows
        corner = jnp.where((key_off >= 0) & (key_off < rows) & (key_off > row_at), DROP, 0.0)
        corner = jnp.concatenate([corner] * GROUP, axis=0)
        for head in range(heads // GROUP):
            for member in range(GROUP):
                local = head * GROUP + member
                line = local % list_rows
                bias = biases[local // list_rows][line : line + 1, :]
                at = slice(member * rows, (member + 1) * rows)
                if side == 0:
                    q_from = pl.multiple_of((core * heads + local) * width, width)
                    q_aug[head, at, :width] = q_own[:, pl.ds(q_from, width)]
                else:
                    q_aug[head, at, :width] = q_other[:, local * width : (local + 1) * width]
                q_aug[head, at, width:] = jnp.broadcast_to(bias, (rows, width)).astype(jnp.bfloat16)
            scores = lax.dot_general(
                q_aug[head], k_aug[head], (((1,), (1,)), ((), ())), preferred_element_type=jnp.float32
            )
            if waiting:
                settle(*waiting)
            waiting = (side, head, scores, corner)
    settle(*waiting)


def far_kernel(z_size, whole, q_aug, total, top, k_far, v_far, target, k_aug, v_aug, *spare):
    width = HEAD_DIMENSION
    rows = target.shape[0]
    out = spare[0] if whole else target
    copies = []
    kv_heads = k_aug.shape[0]
    place = chip_place(z_size) + z_size
    fill_keys(z_size, rows, k_aug, v_aug, 0, place, k_far[...], v_far[...])
    for head in range(kv_heads):
        scores = lax.dot_general(
            q_aug[head], k_aug[head], (((1,), (1,)), ((), ())), preferred_element_type=jnp.float32
        )
        near_max = top[head]
        row_max = jnp.maximum(near_max, jnp.max(scores, axis=1, keepdims=True))
        shrink = jnp.exp2((near_max - row_max) * factor())
        probs = jnp.exp2((scores - row_max) * factor()).astype(jnp.bfloat16)
        added = jnp.dot(probs, v_aug[head], preferred_element_type=jnp.float32)
        mixed = total[head, :, :width] * shrink + added[:, :width]
        sums = total[head, :, width:] * shrink + added[:, width:]
        result = (mixed / sums).astype(jnp.bfloat16)
        for member in range(GROUP):
            column = (head * GROUP + member) * width
            out[:, column : column + width] = result[member * rows : (member + 1) * rows]
        if whole:
            span = GROUP * width
            start = pl.multiple_of((lax.axis_index("core") * kv_heads + head) * span, span)
            copy = pltpu.make_async_copy(
                out.at[:, pl.ds(head * span, span)], target.at[:, pl.ds(start, span)], spare[1].at[head]
            )
            copy.start()
            copies.append(copy)
    for copy in copies:
        copy.wait()


def per_device_ring(z_size, queries, keys, values, block_lists, block_counts):
    del block_counts
    rows = queries.shape[0]
    core = lax.axis_index("core")
    half = keys.shape[1] // 2
    heads = queries.shape[1] // HEAD_DIMENSION // 2
    swap = [(0, 1), (1, 0)]
    ahead, back = ring_steps(z_size)
    axes = ("seq", "x", "core")

    own = core * half
    k_got = lax.ppermute(keys, "core", swap)
    v_got = lax.ppermute(values, "core", swap)
    l_got = lax.ppermute(block_lists, "core", swap)
    lines = [part[:, tile] for part in (block_lists, l_got) for tile in range(block_lists.shape[1])]
    lists = jnp.concatenate(lines, axis=1).astype(jnp.bfloat16)
    lists = jnp.pad(lists, ((0, 0), (0, half - lists.shape[1])))
    def halves(part, got):
        return [lax.dynamic_slice_in_dim(part, own, half, 1), lax.dynamic_slice_in_dim(got, own, half, 1)]

    k_unit = jnp.concatenate(halves(keys, k_got), axis=0)
    v_unit = jnp.concatenate(halves(values, v_got) + [lists], axis=0)
    q_width = heads * HEAD_DIMENSION
    q_sent = lax.dynamic_slice_in_dim(queries, q_width - core * q_width, q_width, 1)
    q_other = lax.ppermute(q_sent, "core", swap)
    k_unit, q_other = lax.optimization_barrier((k_unit, q_other))
    k_ahead, k_back, v_ahead, v_back = [k_unit], [k_unit], [v_unit], [v_unit]
    for _ in range(z_size - 1):
        k_ahead.append(lax.ppermute(k_ahead[-1], axes, ahead))
        v_ahead.append(lax.ppermute(v_ahead[-1], axes, ahead))
        k_back.append(lax.ppermute(k_back[-1], axes, back))
        v_back.append(lax.ppermute(v_back[-1], axes, back))
    unit_rows = 2 * rows
    k_far = lax.ppermute(k_ahead[-1], axes, ahead)
    v_far = lax.ppermute(v_back[-1][:unit_rows], axes, back)
    chips = 2 * z_size
    kv_heads = heads // GROUP
    near_rows = (chips - 1) * unit_rows
    group_rows = GROUP * rows
    wide = 2 * HEAD_DIMENSION
    state = pl.pallas_call(
        functools.partial(near_kernel, z_size, heads),
        out_shape=(
            jax.ShapeDtypeStruct((kv_heads, group_rows, wide), jnp.bfloat16),
            jax.ShapeDtypeStruct((kv_heads, group_rows, wide), jnp.float32),
            jax.ShapeDtypeStruct((kv_heads, group_rows, HEAD_DIMENSION), jnp.float32),
        )
        * 2,
        scratch_shapes=[
            pltpu.VMEM((kv_heads, near_rows, wide), jnp.bfloat16),
            pltpu.VMEM((kv_heads, near_rows, wide), jnp.bfloat16),
            pltpu.VMEM(((chips - 1) * block_lists.shape[0], HEAD_DIMENSION), jnp.float32),
        ],
        compiler_params=pltpu.CompilerParams(vmem_limit_bytes=40 * 2**20),
        cost_estimate=pl.CostEstimate(
            flops=4 * 2 * kv_heads * group_rows * near_rows * wide,
            bytes_accessed=8 * 2**20,
            transcendentals=2 * kv_heads * group_rows * near_rows,
        ),
        name="near",
    )(queries, q_other, *k_ahead, *k_back[1:], *v_ahead, *v_back[1:])

    def finish(side, whole):
        return pl.pallas_call(
            functools.partial(far_kernel, z_size, whole),
            out_shape=jax.ShapeDtypeStruct((rows, q_width * (2 if whole else 1)), jnp.bfloat16),
            out_specs=pl.BlockSpec(memory_space=pl.ANY if whole else pltpu.VMEM),
            scratch_shapes=[
                pltpu.VMEM((kv_heads, unit_rows, wide), jnp.bfloat16),
                pltpu.VMEM((kv_heads, unit_rows, wide), jnp.bfloat16),
            ]
            + ([pltpu.VMEM((rows, q_width), jnp.bfloat16), pltpu.SemaphoreType.DMA((kv_heads,))] if whole else []),
            compiler_params=pltpu.CompilerParams(vmem_limit_bytes=40 * 2**20),
            cost_estimate=pl.CostEstimate(
                flops=4 * kv_heads * group_rows * unit_rows * wide,
                bytes_accessed=8 * 2**20,
                transcendentals=2 * kv_heads * group_rows * unit_rows,
            ),
            name="far_own" if whole else "far_other",
        )(*state[3 * side : 3 * side + 3], k_far, v_far)

    back_home = lax.ppermute(finish(1, False), "core", swap)
    return lax.dynamic_update_slice_in_dim(finish(0, True), back_home, q_width - core * q_width, 1)


def solution(mesh):
    groups, z_size, tiles = (mesh.shape[a] for a in ("groups", "seq", "tile"))
    if tiles == 4 and z_size == 4:
        fine = Mesh(mesh.devices.reshape(groups, z_size, 2, 2), ("groups", "seq", "x", "core"))
        step, tile, on = functools.partial(per_device_ring, z_size), ("x", "core"), fine
    else:
        step, tile, on = per_device, ("tile",), mesh
    rows = P(("groups",) + tile + ("seq",), None)
    in_specs = (
        rows,
        rows,
        rows,
        P(("groups", "seq"), tile, None),
        P(("groups", "seq"), tile),
    )
    return jax.shard_map(step, mesh=on, in_specs=in_specs, out_specs=rows, check_vma=False)
```
